32 devices in a mesh: dp: 8 (over z, core), space: 4 (over y, x).
Axes of the slice: x: 2, y: 2, z: 4, core: 2. Of those that a mesh axis runs over, the one named last changes fastest.
Arguments:
- cotangent: bfloat16 [8, 24, 128, 1024], P('dp', None, 'space'), may hold values from -6 to 6
- spectrum: float32 [64, 8, 24, 128], P('space', 'dp'), may hold values from -6 to 6
- weights: float32 [64, 24, 24, 128], P('space'), may hold values from -0.875 to 0.875
Outputs:
- grad_input: bfloat16 [8, 24, 128, 1024], P('dp', None, 'space')
- grad_weights: float32 [64, 576, 128], P('space', 'dp')
The draws below stay inside these ranges and needn't reach their ends.
All inputs are finite; a program needn't handle non-finite values.
Results may differ from the reference program's by a relative error of at most 0.001.
Values sent between devices are 32-bit elements; how exact they have to be, the bound alone decides.
A program may use at most 64 MiB of HBM per device.

```python
import math
import jax
import jax.numpy as jnp
from jax import lax

C = 24
M1 = 64
M2 = 64
W = 1024
H = 128
BATCH = 8


def levels(stream_key, shape, split, low, top_value):
    def one(axis_at, shards_of):
        steps = jax.random.uniform(jax.random.fold_in(jax.random.fold_in(stream_key, 6), axis_at), (shards_of,), jnp.float32, low / len(split), top_value / len(split))
        return jnp.repeat(jnp.exp(steps), shape[axis_at] // shards_of).reshape((-1,) + (1,) * (len(shape) - axis_at - 1))

    loudness = one(*split[0])
    for cut in split[1:]:
        loudness = loudness * one(*cut)
    return loudness


def scatter_about(own_key, dims, scale, bound, shards=(), held_as=jnp.bfloat16):
    values = scale * jax.random.normal(own_key, dims, jnp.float32)
    if shards:
        values = values * levels(own_key, dims, shards, -0.22, 0.18)
    return jnp.clip(values, -bound, bound).astype(held_as)


def setup_inputs(seed: int = 0) -> dict:
    streams_of = jax.random.split(jax.random.key(seed), 4)
    cotangent = scatter_about(streams_of[0], (BATCH, C, H, W), 1.0, 6.0, ((0, 8), (2, 4)))
    spectrum = scatter_about(streams_of[1], (M1, BATCH, C, 2 * M2), 1.0, 6.0, ((0, 4), (1, 8)), jnp.float32)
    weights = scatter_about(streams_of[2], (M1, C, C, 2 * M2), (2 * C) ** -0.5, 0.875, ((0, 4),), jnp.float32)
    return dict(cotangent=cotangent, spectrum=spectrum, weights=weights)


def column_basis(col_count, modes_y):
    position = jnp.arange(col_count, dtype=jnp.int32)
    frequency = jnp.arange(modes_y, dtype=jnp.int32)
    phase = position[:, None] * frequency[None, :] % col_count
    angles = phase.astype(jnp.float32) * (2.0 * math.pi / col_count)
    return jnp.concatenate([jnp.cos(angles), -jnp.sin(angles)], axis=1)

def row_basis(first_mode, mode_count, first_row, row_count, height):
    frequency = first_mode + jnp.arange(mode_count, dtype=jnp.int32)
    position = first_row + jnp.arange(row_count, dtype=jnp.int32)
    phase = frequency[:, None] * position[None, :] % height
    angles = phase.astype(jnp.float32) * (2.0 * math.pi / height)
    return (jnp.cos(angles), jnp.sin(angles))

def spectral_backward(spec_grad, weights, modes_y):
    hp = lax.Precision.HIGHEST
    grad_re, grad_im = (spec_grad[..., :modes_y], spec_grad[..., modes_y:])
    weight_re, weight_im = (weights[..., :modes_y], weights[..., modes_y:])
    real_part = jnp.einsum('kbox,kcox->kbcx', grad_re, weight_re, precision=hp) + jnp.einsum('kbox,kcox->kbcx', grad_im, weight_im, precision=hp)
    imag_part = jnp.einsum('kbox,kcox->kbcx', grad_im, weight_re, precision=hp) - jnp.einsum('kbox,kcox->kbcx', grad_re, weight_im, precision=hp)
    return jnp.concatenate([real_part, imag_part], axis=-1)

def weight_terms(spectrum, spec_grad, modes_y):
    hp = lax.Precision.HIGHEST
    spec_re, spec_im = (spectrum[..., :modes_y], spectrum[..., modes_y:])
    grad_re, grad_im = (spec_grad[..., :modes_y], spec_grad[..., modes_y:])
    real_part = jnp.einsum('kbcx,kbox->kcox', spec_re, grad_re, precision=hp) + jnp.einsum('kbcx,kbox->kcox', spec_im, grad_im, precision=hp)
    imag_part = jnp.einsum('kbcx,kbox->kcox', spec_re, grad_im, precision=hp) - jnp.einsum('kbcx,kbox->kcox', spec_im, grad_re, precision=hp)
    joined = jnp.concatenate([real_part, imag_part], axis=-1)
    return joined.reshape(joined.shape[0], joined.shape[1] * joined.shape[2], joined.shape[3])

def reference(cotangent, spectrum, weights):
    hp = lax.Precision.HIGHEST
    basis = column_basis(W, M2)

    def column_pass(raster):
        return jnp.einsum('cxw,wj->cxj', raster.astype(jnp.float32), basis, precision=hp)
    col_spec = lax.map(column_pass, cotangent)
    cosines, sines = row_basis(0, M1, 0, H, H)
    forward_scale = 1.0 / math.sqrt(H * W)
    with_cos = jnp.einsum('kx,bcxj->kbcj', cosines, col_spec, precision=hp)
    with_sin = jnp.einsum('kx,bcxj->kbcj', sines, col_spec, precision=hp)
    spec_grad = jnp.concatenate([with_cos[..., :M2] + with_sin[..., M2:], with_cos[..., M2:] - with_sin[..., :M2]], axis=-1) * forward_scale
    input_spec = spectral_backward(spec_grad, weights, M2)
    grad_weights = weight_terms(spectrum, spec_grad, M2)
    back_cos = jnp.einsum('kx,kbcj->bcxj', cosines, input_spec, precision=hp)
    back_sin = jnp.einsum('kx,kbcj->bcxj', sines, input_spec, precision=hp)
    back = jnp.concatenate([back_cos[..., :M2] - back_sin[..., M2:], back_cos[..., M2:] + back_sin[..., :M2]], axis=-1)
    inverse_scale = 1.0 / math.sqrt(M1 * M2)

    def inverse_pass(block):
        return (jnp.einsum('cxj,wj->cxw', block, basis, precision=hp) * inverse_scale).astype(jnp.bfloat16)
    grad_input = lax.map(inverse_pass, back)
    return (grad_input, grad_weights)
```

```python
import functools
import math

import jax
import jax.numpy as jnp
import ml_dtypes
import numpy as np
from jax import lax
from jax.experimental import pallas as pl
from jax.experimental.pallas import tpu as pltpu
from jax.sharding import PartitionSpec as P

MESH = pl.DeviceIdType.MESH
GROUP = 8


def column_basis(col_count, modes_y):
    position = jnp.arange(col_count, dtype=jnp.int32)
    frequency = jnp.arange(modes_y, dtype=jnp.int32)
    phase = position[:, None] * frequency[None, :] % col_count
    angles = phase.astype(jnp.float32) * (2.0 * math.pi / col_count)
    return jnp.concatenate([jnp.cos(angles), -jnp.sin(angles)], axis=1)


def row_basis(mode_count, first_row, row_count, height):
    frequency = jnp.arange(mode_count, dtype=jnp.int32)
    position = first_row + jnp.arange(row_count, dtype=jnp.int32)
    phase = frequency[:, None] * position[None, :] % height
    angles = phase.astype(jnp.float32) * (2.0 * math.pi / height)
    return (jnp.cos(angles), jnp.sin(angles))


def spectral_backward(spec_grad, weights, modes_y):
    hp = lax.Precision.HIGHEST
    grad_re, grad_im = (spec_grad[..., :modes_y], spec_grad[..., modes_y:])
    weight_re, weight_im = (weights[..., :modes_y], weights[..., modes_y:])
    real_part = jnp.einsum("kbox,kcox->kbcx", grad_re, weight_re, precision=hp) + jnp.einsum(
        "kbox,kcox->kbcx", grad_im, weight_im, precision=hp
    )
    imag_part = jnp.einsum("kbox,kcox->kbcx", grad_im, weight_re, precision=hp) - jnp.einsum(
        "kbox,kcox->kbcx", grad_re, weight_im, precision=hp
    )
    return jnp.concatenate([real_part, imag_part], axis=-1)


def weight_terms(spectrum, spec_grad, modes_y):
    hp = lax.Precision.HIGHEST
    spec_re, spec_im = (spectrum[..., :modes_y], spectrum[..., modes_y:])
    grad_re, grad_im = (spec_grad[..., :modes_y], spec_grad[..., modes_y:])
    real_part = jnp.einsum("kbcx,kbox->kcox", spec_re, grad_re, precision=hp) + jnp.einsum(
        "kbcx,kbox->kcox", spec_im, grad_im, precision=hp
    )
    imag_part = jnp.einsum("kbcx,kbox->kcox", spec_re, grad_im, precision=hp) - jnp.einsum(
        "kbcx,kbox->kcox", spec_im, grad_re, precision=hp
    )
    joined = jnp.concatenate([real_part, imag_part], axis=-1)
    return joined.reshape(joined.shape[0], joined.shape[1] * joined.shape[2], joined.shape[3])


def general_body(cotangent, spectrum, weights):
    hp = lax.Precision.HIGHEST
    space_count = lax.axis_size("space")
    raster_count, channels, row_count, col_count = cotangent.shape
    local_modes = spectrum.shape[0]
    modes_y = spectrum.shape[3] // 2
    height = row_count * space_count
    basis = column_basis(col_count, modes_y)
    first_row = lax.axis_index("space") * row_count
    col_spec = jnp.einsum(
        "rcxw,wj->rcxj", cotangent, basis, precision=hp, preferred_element_type=jnp.float32
    )
    forward_scale = 1.0 / math.sqrt(height * col_count)
    cosines, sines = row_basis(local_modes * lax.axis_size("space"), first_row, row_count, height)
    with_cos = jnp.einsum("kx,rcxj->krcj", cosines, col_spec, precision=hp)
    with_sin = jnp.einsum("kx,rcxj->krcj", sines, col_spec, precision=hp)
    joined = jnp.concatenate(
        [
            with_cos[..., :modes_y] + with_sin[..., modes_y:],
            with_cos[..., modes_y:] - with_sin[..., :modes_y],
        ],
        axis=-1,
    )
    spec_grad = lax.psum_scatter(joined * forward_scale, "space", scatter_dimension=0, tiled=True)
    input_spec = spectral_backward(spec_grad, weights, modes_y)
    local_terms = weight_terms(spectrum, spec_grad, modes_y)
    grad_weights = lax.psum_scatter(local_terms, "dp", scatter_dimension=1, tiled=True)
    shard_piece = lax.all_gather(input_spec, "space", axis=0, tiled=True)
    cosines, sines = row_basis(shard_piece.shape[0], first_row, row_count, height)
    back_cos = jnp.einsum("kx,krcj->rcxj", cosines, shard_piece, precision=hp)
    back_sin = jnp.einsum("kx,krcj->rcxj", sines, shard_piece, precision=hp)
    joined = jnp.concatenate(
        [
            back_cos[..., :modes_y] - back_sin[..., modes_y:],
            back_cos[..., modes_y:] + back_sin[..., :modes_y],
        ],
        axis=-1,
    )
    inverse_scale = 1.0 / math.sqrt(local_modes * space_count * modes_y)
    grad_input = (jnp.einsum("rcxj,wj->rcxw", joined, basis, precision=hp) * inverse_scale).astype(
        jnp.bfloat16
    )
    return (grad_input, grad_weights)


def halves(table):
    high = table.astype(ml_dtypes.bfloat16)
    low = (table - high.astype(np.float64)).astype(ml_dtypes.bfloat16)
    return high, low


def tables(modes, modes_y, rows, cols, space):
    height = rows * space
    angle = 2.0 * np.pi * (np.outer(np.arange(cols), np.arange(modes_y)) % cols) / cols
    high, low = halves(np.concatenate([np.cos(angle), -np.sin(angle)], axis=1))
    into = np.concatenate([high, low], axis=1)
    out_of = np.concatenate([high.T, high.T, low.T], axis=0)
    angle = 2.0 * np.pi * (np.outer(np.arange(modes), np.arange(height)) % height) / height
    cosines = np.cos(angle).reshape(modes, space, rows).transpose(1, 0, 2)
    sines = np.sin(angle).reshape(modes, space, rows).transpose(1, 0, 2)
    high, low = halves(np.concatenate([cosines, sines], axis=2) / math.sqrt(height * cols))
    rows_in = np.concatenate([high, low, high], axis=2)
    both = np.concatenate([cosines, sines], axis=1).transpose(0, 2, 1)
    high, low = halves(both / math.sqrt(modes * modes_y))
    rows_out = np.concatenate([high, low, high], axis=2)
    return into, rows_in, rows_out, out_of


def split(values):
    high = values.astype(jnp.bfloat16)
    low = (values - high.astype(jnp.float32)).astype(jnp.bfloat16)
    return high, low


def kernel(
    dp, space,
    cot_hbm, spec_hbm, w_hbm, into_hbm, rows_in_hbm, rows_out_hbm, out_of_hbm,
    gin_ref, gw_ref,
    cot, spec, w, into, rows_in, rows_out, out_of,
    part, rs_in, gall, iall, sp_out, sp_in, a_rows, b_rows,
    load_sem, rs_send, rs_recv, ag_send, ag_recv, sp_send, sp_recv,
    up_send, down_send, sib_send, g_recv,
):
    me_d = lax.axis_index("dp")
    me_s = lax.axis_index("space")
    channels, rows, cols = cot.shape
    local = w.shape[0]
    modes = local * space
    lanes = w.shape[3]
    half = lanes // 2
    own = channels // dp
    groups = channels // GROUP

    def at(d, s):
        return {"dp": d, "space": s}

    def partner_d(t):
        return lax.rem(me_d + t, dp)

    def partner_s(t):
        return lax.rem(me_s + t, space)

    def source_s(t):
        return lax.rem(me_s + space - t, space)

    barrier = pltpu.get_barrier_semaphore()
    for t in range(1, dp):
        pl.semaphore_signal(barrier, inc=1, device_id=at(partner_d(t), me_s), device_id_type=MESH)
    for t in range(1, space):
        pl.semaphore_signal(barrier, inc=1, device_id=at(me_d, partner_s(t)), device_id_type=MESH)

    def load(n, src, dst):
        copy = pltpu.make_async_copy(src, dst, load_sem.at[n])
        copy.start()
        return copy

    l_into = load(0, into_hbm, into)
    l_cot = []
    for g in range(groups):
        place = pl.ds(g * GROUP, GROUP)
        l_cot.append(load(1 + g, cot_hbm.at[0, place], cot.at[place]))
    n = 1 + groups
    l_rows_in = load(n, rows_in_hbm.at[me_s], rows_in)
    l_spec = load(n + 1, spec_hbm.at[:, 0], spec)
    l_w = load(n + 2, w_hbm, w)
    l_rows_out = load(n + 3, rows_out_hbm.at[me_s], rows_out)
    l_out_of = load(n + 4, out_of_hbm, out_of)

    lane = lax.broadcasted_iota(jnp.int32, (1, lanes), 1)
    lower = lane < half
    sign = jnp.where(lower, 1.0, -1.0).astype(jnp.float32)

    def turn(values):
        return pltpu.roll(values, half, values.ndim - 1)

    def rs_copy(t, g):
        there = partner_s(t)
        place = pl.ds(g * GROUP, GROUP)
        return pltpu.make_async_remote_copy(
            part.at[pl.ds(there * local, local), place],
            rs_in.at[t - 1, :, place],
            rs_send.at[t - 1, g],
            rs_recv.at[t - 1, g],
            device_id=at(me_d, there),
            device_id_type=MESH,
        )

    def sp_copy(t):
        there = partner_d(t)
        return pltpu.make_async_remote_copy(
            sp_out.at[there],
            sp_in.at[me_d],
            sp_send.at[t],
            sp_recv.at[t],
            device_id=at(there, me_s),
            device_id_type=MESH,
        )

    def sp_arrival(t):
        source = lax.rem(me_d + dp - t, dp)
        return pltpu.make_async_remote_copy(
            sp_out.at[source],
            sp_in.at[source],
            sp_send.at[t],
            sp_recv.at[t],
            device_id=at(source, me_s),
            device_id_type=MESH,
        )

    l_into.wait()
    l_rows_in.wait()
    for g in range(groups):
        l_cot[g].wait()
        block = cot[pl.ds(g * GROUP, GROUP)].reshape(GROUP * rows, cols)
        both = jnp.dot(block, into[...], preferred_element_type=jnp.float32)
        col = both[:, :lanes] + both[:, lanes:]
        turned = turn(col) * sign
        stacked = jnp.concatenate(
            [
                jnp.concatenate(
                    [col[i * rows : (i + 1) * rows], turned[i * rows : (i + 1) * rows]], axis=0
                )
                for i in range(GROUP)
            ],
            axis=1,
        )
        high, low = split(stacked)
        spectrum_part = jnp.dot(
            rows_in[...],
            jnp.concatenate([high, high, low], axis=0),
            preferred_element_type=jnp.float32,
        )
        for i in range(GROUP):
            part[:, g * GROUP + i, :] = spectrum_part[:, i * lanes : (i + 1) * lanes]
        if g == 0:
            pl.semaphore_wait(barrier, dp + space - 2)
        for t in range(1, space):
            rs_copy(t, g).start()

    l_spec.wait()
    for d in range(dp):
        for k in range(local):
            sp_out[d, k * own : (k + 1) * own, :] = spec[k, d * own : (d + 1) * own, :]
    for t in range(1, dp):
        sp_copy(t).start()
    sp_in[me_d] = sp_out[me_d]
    gw_ref[...] = jnp.zeros_like(gw_ref)

    for t in range(1, space):
        for g in range(groups):
            rs_copy(t, g).wait_recv()

    def gather_sum(k, carry):
        total = part[me_s * local + k]
        for t in range(1, space):
            total = total + rs_in[t - 1, k]
        gall[me_d, k] = total
        return carry

    lax.fori_loop(0, local, gather_sum, 0)

    z, core = me_d // 2, lax.rem(me_d, 2)
    nz = dp // 2

    def g_copy(b, there, sem):
        return pltpu.make_async_remote_copy(
            gall.at[b],
            gall.at[b],
            sem.at[b],
            g_recv.at[b],
            device_id=at(there, me_s),
            device_id_type=MESH,
        )

    def up(b):
        return g_copy(b, me_d + 2, up_send)

    def down(b):
        return g_copy(b, me_d - 2, down_send)

    def sibling(b):
        return g_copy(b, me_d + 1 - 2 * core, sib_send)

    @pl.when(z < nz - 1)
    def _():
        up(me_d).start()

    @pl.when(z > 0)
    def _():
        down(me_d).start()

    sibling(me_d).start()

    parts = 2 if local % 2 == 0 else 1
    size = local // parts

    def ag_copy(t, h):
        place = pl.ds(me_s * local + h * size, size)
        return pltpu.make_async_remote_copy(
            iall.at[place],
            iall.at[place],
            ag_send.at[t - 1, h],
            ag_recv.at[t - 1, h],
            device_id=at(me_d, partner_s(t)),
            device_id_type=MESH,
        )

    def ag_arrival(t, h):
        place = pl.ds(source_s(t) * local + h * size, size)
        return pltpu.make_async_remote_copy(
            iall.at[place],
            iall.at[place],
            ag_send.at[t - 1, h],
            ag_recv.at[t - 1, h],
            device_id=at(me_d, source_s(t)),
            device_id_type=MESH,
        )

    def mix(k, carry):
        grad = gall[me_d, k]
        weight = w[k]
        plain = jnp.sum(weight * grad[None], axis=1)
        cross = jnp.sum(weight * turn(grad)[None], axis=1)
        iall[me_s * local + k] = jnp.where(lower, plain + turn(plain), turn(cross) - cross)
        return carry

    l_w.wait()
    for h in range(parts):
        lax.fori_loop(h * size, (h + 1) * size, mix, 0)
        for t in range(1, space):
            ag_copy(t, h).start()

    for t in range(1, dp):
        sp_arrival(t).wait_recv()

    def add_terms(b):
        saved = sp_in[b]
        a_rows[...] = jnp.where(lower, saved, turn(saved))
        b_rows[...] = jnp.where(lower, turn(saved), -saved)

        def one(k, carry):
            grad = gall[b, k]
            turned = turn(grad)
            for c in range(own):
                row = pl.ds(k * own + c, 1)
                place = pl.ds(c * channels, channels)
                gw_ref[k, place, :] += a_rows[row, :] * grad + b_rows[row, :] * turned
            return carry

        lax.fori_loop(0, local, one, 0)

    add_terms(me_d)
    g_copy(me_d + 1 - 2 * core, me_d, sib_send).wait_recv()
    add_terms(me_d + 1 - 2 * core)

    def step(t):
        below, above = me_d - 2 * t, me_d + 2 * t

        @pl.when(z >= t)
        def _():
            down(below).wait_recv()

            @pl.when(z < nz - 1)
            def _():
                up(below).start()

            sibling(below).start()

        @pl.when(z + t < nz)
        def _():
            up(above).wait_recv()

            @pl.when(z > 0)
            def _():
                down(above).start()

            sibling(above).start()

        @pl.when(z >= t)
        def _():
            add_terms(below)
            other = below + 1 - 2 * core
            sibling(other).wait_recv()
            add_terms(other)

        @pl.when(z + t < nz)
        def _():
            add_terms(above)
            other = above + 1 - 2 * core
            sibling(other).wait_recv()
            add_terms(other)

    def back_transform():
        l_rows_out.wait()
        l_out_of.wait()
        for t in range(1, space):
            for h in range(parts):
                ag_arrival(t, h).wait_recv()
        for g in range(groups):
            mixed = jnp.concatenate(
                [iall[:, g * GROUP + i, :] for i in range(GROUP)], axis=1
            )
            turned = jnp.concatenate(
                [
                    -sign * turn(mixed[:, i * lanes : (i + 1) * lanes])
                    for i in range(GROUP)
                ],
                axis=1,
            )
            high, low = split(jnp.concatenate([mixed, turned], axis=0))
            back = jnp.dot(
                rows_out[...],
                jnp.concatenate([high, high, low], axis=0),
                preferred_element_type=jnp.float32,
            )
            back = jnp.concatenate(
                [back[:, i * lanes : (i + 1) * lanes] for i in range(GROUP)], axis=0
            )
            high, low = split(back)
            raster = jnp.dot(
                jnp.concatenate([high, low, high], axis=1),
                out_of[...],
                preferred_element_type=jnp.float32,
            )
            gin_ref[0, pl.ds(g * GROUP, GROUP)] = raster.reshape(GROUP, rows, cols).astype(
                jnp.bfloat16
            )

    for t in range(1, nz):
        if t == nz - 1:
            back_transform()
        step(t)

    for t in range(1, space):
        for g in range(groups):
            rs_copy(t, g).wait_send()
        for h in range(parts):
            ag_copy(t, h).wait_send()
    for t in range(1, dp):
        sp_copy(t).wait_send()
    sibling(me_d).wait_send()

    @pl.when(z < nz - 1)
    def _():
        up(me_d).wait_send()

    @pl.when(z > 0)
    def _():
        down(me_d).wait_send()

    for t in range(1, nz):

        @pl.when(z >= t)
        def _():
            @pl.when(z < nz - 1)
            def _():
                up(me_d - 2 * t).wait_send()

            sibling(me_d - 2 * t).wait_send()

        @pl.when(z + t < nz)
        def _():
            @pl.when(z > 0)
            def _():
                down(me_d + 2 * t).wait_send()

            sibling(me_d + 2 * t).wait_send()


def fused_body(dp, space, cotangent, spectrum, weights):
    _, channels, rows, cols = cotangent.shape
    local, _, _, lanes = spectrum.shape
    modes = local * space
    own = channels // dp
    groups = channels // GROUP
    fixed = [jnp.asarray(t) for t in tables(modes, lanes // 2, rows, cols, space)]
    into, rows_in, rows_out, out_of = fixed
    f32 = jnp.float32
    dma = pltpu.SemaphoreType.DMA
    return pl.pallas_call(
        functools.partial(kernel, dp, space),
        out_shape=(
            jax.ShapeDtypeStruct(cotangent.shape, jnp.bfloat16),
            jax.ShapeDtypeStruct((local, own * channels, lanes), f32),
        ),
        in_specs=[pl.BlockSpec(memory_space=pl.ANY)] * 7,
        out_specs=[pl.BlockSpec(memory_space=pltpu.VMEM)] * 2,
        scratch_shapes=[
            pltpu.VMEM((channels, rows, cols), jnp.bfloat16),
            pltpu.VMEM((local, channels, lanes), f32),
            pltpu.VMEM(weights.shape, f32),
            pltpu.VMEM(into.shape, jnp.bfloat16),
            pltpu.VMEM(rows_in.shape[1:], jnp.bfloat16),
            pltpu.VMEM(rows_out.shape[1:], jnp.bfloat16),
            pltpu.VMEM(out_of.shape, jnp.bfloat16),
            pltpu.VMEM((modes, channels, lanes), f32),
            pltpu.VMEM((space - 1, local, channels, lanes), f32),
            pltpu.VMEM((dp, local, channels, lanes), f32),
            pltpu.VMEM((modes, channels, lanes), f32),
            pltpu.VMEM((dp, local * own, lanes), f32),
            pltpu.VMEM((dp, local * own, lanes), f32),
            pltpu.VMEM((local * own, lanes), f32),
            pltpu.VMEM((local * own, lanes), f32),
            dma((groups + 6,)),
            dma((space - 1, groups)),
            dma((space - 1, groups)),
            dma((space - 1, 2)),
            dma((space - 1, 2)),
            dma((dp,)),
            dma((dp,)),
            dma((dp,)),
            dma((dp,)),
            dma((dp,)),
            dma((dp,)),
        ],
        compiler_params=pltpu.CompilerParams(
            collective_id=0, has_side_effects=True, vmem_limit_bytes=48 * 1024 * 1024
        ),
    )(cotangent, spectrum, weights, into, rows_in, rows_out, out_of)


def solution(mesh):
    placed = (
        P("dp", None, "space", None),
        P("space", "dp", None, None),
        P("space", None, None, None),
    )
    dp, space = mesh.shape["dp"], mesh.shape["space"]

    def body(cotangent, spectrum, weights):
        rasters, channels, rows, _ = cotangent.shape
        whole_rows = (
            rasters == 1
            and dp % 2 == 0
            and channels % dp == 0
            and channels % GROUP == 0
            and rows % 16 == 0
            and (spectrum.shape[0] * (channels // dp)) % 8 == 0
        )
        if whole_rows:
            return fused_body(dp, space, cotangent, spectrum, weights)
        return general_body(cotangent, spectrum, weights)

    return jax.shard_map(
        body,
        mesh=mesh,
        in_specs=placed,
        out_specs=(P("dp", None, "space", None), P("space", "dp", None)),
        check_vma=False,
    )
```

```python
import functools
import math

import jax
import jax.numpy as jnp
import ml_dtypes
import numpy as np
from jax import lax
from jax.experimental import pallas as pl
from jax.experimental.pallas import tpu as pltpu
from jax.sharding import PartitionSpec as P

MESH = pl.DeviceIdType.MESH
GROUP = 8


def column_basis(col_count, modes_y):
    position = jnp.arange(col_count, dtype=jnp.int32)
    frequency = jnp.arange(modes_y, dtype=jnp.int32)
    phase = position[:, None] * frequency[None, :] % col_count
    angles = phase.astype(jnp.float32) * (2.0 * math.pi / col_count)
    return jnp.concatenate([jnp.cos(angles), -jnp.sin(angles)], axis=1)


def row_basis(mode_count, first_row, row_count, height):
    frequency = jnp.arange(mode_count, dtype=jnp.int32)
    position = first_row + jnp.arange(row_count, dtype=jnp.int32)
    phase = frequency[:, None] * position[None, :] % height
    angles = phase.astype(jnp.float32) * (2.0 * math.pi / height)
    return (jnp.cos(angles), jnp.sin(angles))


def spectral_backward(spec_grad, weights, modes_y):
    hp = lax.Precision.HIGHEST
    grad_re, grad_im = (spec_grad[..., :modes_y], spec_grad[..., modes_y:])
    weight_re, weight_im = (weights[..., :modes_y], weights[..., modes_y:])
    real_part = jnp.einsum("kbox,kcox->kbcx", grad_re, weight_re, precision=hp) + jnp.einsum(
        "kbox,kcox->kbcx", grad_im, weight_im, precision=hp
    )
    imag_part = jnp.einsum("kbox,kcox->kbcx", grad_im, weight_re, precision=hp) - jnp.einsum(
        "kbox,kcox->kbcx", grad_re, weight_im, precision=hp
    )
    return jnp.concatenate([real_part, imag_part], axis=-1)


def weight_terms(spectrum, spec_grad, modes_y):
    hp = lax.Precision.HIGHEST
    spec_re, spec_im = (spectrum[..., :modes_y], spectrum[..., modes_y:])
    grad_re, grad_im = (spec_grad[..., :modes_y], spec_grad[..., modes_y:])
    real_part = jnp.einsum("kbcx,kbox->kcox", spec_re, grad_re, precision=hp) + jnp.einsum(
        "kbcx,kbox->kcox", spec_im, grad_im, precision=hp
    )
    imag_part = jnp.einsum("kbcx,kbox->kcox", spec_re, grad_im, precision=hp) - jnp.einsum(
        "kbcx,kbox->kcox", spec_im, grad_re, precision=hp
    )
    joined = jnp.concatenate([real_part, imag_part], axis=-1)
    return joined.reshape(joined.shape[0], joined.shape[1] * joined.shape[2], joined.shape[3])


def general_body(cotangent, spectrum, weights):
    hp = lax.Precision.HIGHEST
    space_count = lax.axis_size("space")
    raster_count, channels, row_count, col_count = cotangent.shape
    local_modes = spectrum.shape[0]
    modes_y = spectrum.shape[3] // 2
    height = row_count * space_count
    basis = column_basis(col_count, modes_y)
    first_row = lax.axis_index("space") * row_count
    col_spec = jnp.einsum(
        "rcxw,wj->rcxj", cotangent, basis, precision=hp, preferred_element_type=jnp.float32
    )
    forward_scale = 1.0 / math.sqrt(height * col_count)
    cosines, sines = row_basis(local_modes * lax.axis_size("space"), first_row, row_count, height)
    with_cos = jnp.einsum("kx,rcxj->krcj", cosines, col_spec, precision=hp)
    with_sin = jnp.einsum("kx,rcxj->krcj", sines, col_spec, precision=hp)
    joined = jnp.concatenate(
        [
            with_cos[..., :modes_y] + with_sin[..., modes_y:],
            with_cos[..., modes_y:] - with_sin[..., :modes_y],
        ],
        axis=-1,
    )
    spec_grad = lax.psum_scatter(joined * forward_scale, "space", scatter_dimension=0, tiled=True)
    input_spec = spectral_backward(spec_grad, weights, modes_y)
    local_terms = weight_terms(spectrum, spec_grad, modes_y)
    grad_weights = lax.psum_scatter(local_terms, "dp", scatter_dimension=1, tiled=True)
    shard_piece = lax.all_gather(input_spec, "space", axis=0, tiled=True)
    cosines, sines = row_basis(shard_piece.shape[0], first_row, row_count, height)
    back_cos = jnp.einsum("kx,krcj->rcxj", cosines, shard_piece, precision=hp)
    back_sin = jnp.einsum("kx,krcj->rcxj", sines, shard_piece, precision=hp)
    joined = jnp.concatenate(
        [
            back_cos[..., :modes_y] - back_sin[..., modes_y:],
            back_cos[..., modes_y:] + back_sin[..., :modes_y],
        ],
        axis=-1,
    )
    inverse_scale = 1.0 / math.sqrt(local_modes * space_count * modes_y)
    grad_input = (jnp.einsum("rcxj,wj->rcxw", joined, basis, precision=hp) * inverse_scale).astype(
        jnp.bfloat16
    )
    return (grad_input, grad_weights)


def halves(table):
    high = table.astype(ml_dtypes.bfloat16)
    low = (table - high.astype(np.float64)).astype(ml_dtypes.bfloat16)
    return high, low


def tables(modes, modes_y, rows, cols, space):
    height = rows * space
    angle = 2.0 * np.pi * (np.outer(np.arange(cols), np.arange(modes_y)) % cols) / cols
    high, low = halves(np.concatenate([np.cos(angle), -np.sin(angle)], axis=1))
    into = np.concatenate([high, low], axis=1)
    out_of = np.concatenate([high.T, high.T, low.T], axis=0)
    angle = 2.0 * np.pi * (np.outer(np.arange(modes), np.arange(height)) % height) / height
    cosines = np.cos(angle).reshape(modes, space, rows).transpose(1, 0, 2)
    sines = np.sin(angle).reshape(modes, space, rows).transpose(1, 0, 2)
    high, low = halves(np.concatenate([cosines, sines], axis=2) / math.sqrt(height * cols))
    rows_in = np.concatenate([high, low, high], axis=2)
    local = modes // space
    order = np.arange(modes).reshape(space, 2, local // 2).transpose(1, 0, 2).reshape(2, -1)
    both = np.concatenate([cosines[:, order], sines[:, order]], axis=2).transpose(0, 1, 3, 2)
    high, low = halves(both / math.sqrt(modes * modes_y))
    rows_out = np.concatenate([high, low, high], axis=3)
    return into, rows_in, rows_out, out_of


def split(values):
    high = values.astype(jnp.bfloat16)
    low = (values - high.astype(jnp.float32)).astype(jnp.bfloat16)
    return high, low


def kernel(
    dp, space,
    cot_hbm, spec_hbm, w_hbm, into_hbm, rows_in_hbm, rows_out_hbm, out_of_hbm,
    gin_hbm, gw_hbm,
    gin_ref, gw_ref, cot, spec, w, into, rows_in, rows_out, out_of,
    part, rs_in, gall, iall, back_sum, sp_out, sp_in, a_rows, b_rows,
    load_sem, store_sem, rs_send, rs_recv, ag_send, ag_recv, sp_send, sp_recv,
    up_send, down_send, sib_send, g_recv,
):
    me_d = lax.axis_index("dp")
    me_s = lax.axis_index("space")
    channels, rows, cols = cot.shape
    local = w.shape[0]
    modes = local * space
    lanes = w.shape[3]
    half = lanes // 2
    own = channels // dp
    groups = channels // GROUP

    def at(d, s):
        return {"dp": d, "space": s}

    def partner_d(t):
        return lax.rem(me_d + t, dp)

    def partner_s(t):
        return lax.rem(me_s + t, space)

    def source_s(t):
        return lax.rem(me_s + space - t, space)

    barrier = pltpu.get_barrier_semaphore()
    for t in range(1, dp):
        pl.semaphore_signal(barrier, inc=1, device_id=at(partner_d(t), me_s), device_id_type=MESH)
    for t in range(1, space):
        pl.semaphore_signal(barrier, inc=1, device_id=at(me_d, partner_s(t)), device_id_type=MESH)

    def load(n, src, dst):
        copy = pltpu.make_async_copy(src, dst, load_sem.at[n])
        copy.start()
        return copy

    l_into = load(0, into_hbm, into)
    l_cot = []
    for g in range(groups):
        place = pl.ds(g * GROUP, GROUP)
        l_cot.append(load(1 + g, cot_hbm.at[0, place], cot.at[place]))
    n = 1 + groups
    l_rows_in = load(n, rows_in_hbm.at[me_s], rows_in)
    l_spec = load(n + 1, spec_hbm.at[:, 0], spec)
    l_w = load(n + 2, w_hbm, w)
    l_rows_out = load(n + 3, rows_out_hbm.at[me_s], rows_out)
    l_out_of = load(n + 4, out_of_hbm, out_of)

    lane = lax.broadcasted_iota(jnp.int32, (1, lanes), 1)
    lower = lane < half
    sign = jnp.where(lower, 1.0, -1.0).astype(jnp.float32)

    def turn(values):
        return pltpu.roll(values, half, values.ndim - 1)

    size = local // 2

    def rs_copy(t, piece):
        there = partner_s(t)
        if piece < groups:
            first, place = 0, pl.ds(piece * GROUP, GROUP)
        else:
            first, place = size, pl.ds(0, channels)
        return pltpu.make_async_remote_copy(
            part.at[pl.ds(there * local + first, size), place],
            rs_in.at[t - 1, pl.ds(first, size), place],
            rs_send.at[t - 1, piece],
            rs_recv.at[t - 1, piece],
            device_id=at(me_d, there),
            device_id_type=MESH,
        )

    def sp_copy(t):
        there = partner_d(t)
        return pltpu.make_async_remote_copy(
            sp_out.at[there],
            sp_in.at[me_d],
            sp_send.at[t],
            sp_recv.at[t],
            device_id=at(there, me_s),
            device_id_type=MESH,
        )

    def sp_arrival(t):
        source = lax.rem(me_d + dp - t, dp)
        return pltpu.make_async_remote_copy(
            sp_out.at[source],
            sp_in.at[source],
            sp_send.at[t],
            sp_recv.at[t],
            device_id=at(source, me_s),
            device_id_type=MESH,
        )

    l_into.wait()
    l_rows_in.wait()
    for g in range(groups):
        l_cot[g].wait()
        block = cot[pl.ds(g * GROUP, GROUP)].reshape(GROUP * rows, cols)
        both = jnp.dot(block, into[...], preferred_element_type=jnp.float32)
        col = both[:, :lanes] + both[:, lanes:]
        turned = turn(col) * sign
        stacked = jnp.concatenate(
            [
                jnp.concatenate(
                    [col[i * rows : (i + 1) * rows], turned[i * rows : (i + 1) * rows]], axis=0
                )
                for i in range(GROUP)
            ],
            axis=1,
        )
        high, low = split(stacked)
        spectrum_part = jnp.dot(
            rows_in[...],
            jnp.concatenate([high, high, low], axis=0),
            preferred_element_type=jnp.float32,
        )
        for i in range(GROUP):
            part[:, g * GROUP + i, :] = spectrum_part[:, i * lanes : (i + 1) * lanes]
        if g == 0:
            pl.semaphore_wait(barrier, dp + space - 2)
        for t in range(1, space):
            rs_copy(t, g).start()
    for t in range(1, space):
        rs_copy(t, groups).start()

    l_spec.wait()
    for d in range(dp):
        for k in range(local):
            sp_out[d, k * own : (k + 1) * own, :] = spec[k, d * own : (d + 1) * own, :]
    for t in range(1, dp):
        sp_copy(t).start()
    sp_in[me_d] = sp_out[me_d]
    gw_ref[...] = jnp.zeros_like(gw_ref)

    z, core = me_d // 2, lax.rem(me_d, 2)
    nz = dp // 2
    twin = 1 - 2 * core

    def g_copy(b, h, there, sem):
        place = pl.ds(h * size, size)
        return pltpu.make_async_remote_copy(
            gall.at[b, place],
            gall.at[b, place],
            sem.at[b, h],
            g_recv.at[b, h],
            device_id=at(there, me_s),
            device_id_type=MESH,
        )

    def up(b, h):
        return g_copy(b, h, me_d + 2, up_send)

    def down(b, h):
        return g_copy(b, h, me_d - 2, down_send)

    def sibling(b, h):
        return g_copy(b, h, me_d + twin, sib_send)

    def own_sends(h, act):
        @pl.when(z < nz - 1)
        def _():
            act(up(me_d, h))

        @pl.when(z > 0)
        def _():
            act(down(me_d, h))

        act(sibling(me_d, h))

    def passed_on(t, h, act, arrive):
        @pl.when(z >= t)
        def _():
            below = me_d - 2 * t
            if arrive:
                down(below, h).wait_recv()

            @pl.when(z < nz - 1)
            def _():
                act(up(below, h))

            act(sibling(below, h))

        @pl.when(z + t < nz)
        def _():
            above = me_d + 2 * t
            if arrive:
                up(above, h).wait_recv()

            @pl.when(z > 0)
            def _():
                act(down(above, h))

            act(sibling(above, h))

    def forward(t, h):
        passed_on(t, h, lambda copy: copy.start(), True)

    def ag_copy(t, h):
        place = pl.ds(me_s * size, size)
        return pltpu.make_async_remote_copy(
            iall.at[h, place],
            iall.at[h, place],
            ag_send.at[t - 1, h],
            ag_recv.at[t - 1, h],
            device_id=at(me_d, partner_s(t)),
            device_id_type=MESH,
        )

    def ag_arrival(t, h):
        place = pl.ds(source_s(t) * size, size)
        return pltpu.make_async_remote_copy(
            iall.at[h, place],
            iall.at[h, place],
            ag_send.at[t - 1, h],
            ag_recv.at[t - 1, h],
            device_id=at(me_d, source_s(t)),
            device_id_type=MESH,
        )

    def sum_and_mix(h):
        for t in range(1, space):
            for piece in range(groups) if h == 0 else (groups,):
                rs_copy(t, piece).wait_recv()

        def gather_sum(k, carry):
            total = part[me_s * local + k]
            for t in range(1, space):
                total = total + rs_in[t - 1, k]
            gall[me_d, k] = total
            return carry

        lax.fori_loop(h * size, (h + 1) * size, gather_sum, 0)
        own_sends(h, lambda copy: copy.start())
        if h == 0:
            l_w.wait()

        def mix(k, carry):
            grad = gall[me_d, k]
            weight = w[k]
            plain = jnp.sum(weight * grad[None], axis=1)
            cross = jnp.sum(weight * turn(grad)[None], axis=1)
            mixed = jnp.where(lower, plain + turn(plain), turn(cross) - cross)
            iall[h, me_s * size + k - h * size] = mixed
            return carry

        lax.fori_loop(h * size, (h + 1) * size, mix, 0)
        for t in range(1, space):
            ag_copy(t, h).start()

    def rows_of(b):
        saved = sp_in[b]
        a_rows[b] = jnp.where(lower, saved, turn(saved))
        b_rows[b] = jnp.where(lower, turn(saved), -saved)

    def add_terms(b, h):
        def one(k, carry):
            grad = gall[b, k]
            turned = turn(grad)
            for c in range(own):
                row = pl.ds(k * own + c, 1)
                place = pl.ds(c * channels, channels)
                gw_ref[k, place, :] += a_rows[b, row, :] * grad + b_rows[b, row, :] * turned
            return carry

        lax.fori_loop(h * size, (h + 1) * size, one, 0)

    def pair_terms(b, h):
        add_terms(b, h)
        sibling(b + twin, h).wait_recv()
        add_terms(b + twin, h)

    def terms(t, h):
        @pl.when(z >= t)
        def _():
            pair_terms(me_d - 2 * t, h)

        @pl.when(z + t < nz)
        def _():
            pair_terms(me_d + 2 * t, h)

    def rows_back(h):
        for t in range(1, space):
            ag_arrival(t, h).wait_recv()
        for g in range(groups):
            mixed = jnp.concatenate([iall[h, :, g * GROUP + i, :] for i in range(GROUP)], axis=1)
            turned = jnp.concatenate(
                [-sign * turn(mixed[:, i * lanes : (i + 1) * lanes]) for i in range(GROUP)],
                axis=1,
            )
            high, low = split(jnp.concatenate([mixed, turned], axis=0))
            found = jnp.dot(
                rows_out[h],
                jnp.concatenate([high, high, low], axis=0),
                preferred_element_type=jnp.float32,
            )
            place = pl.ds(g * GROUP * lanes, GROUP * lanes)
            if h == 0:
                back_sum[:, place] = found
            else:
                columns_back(g, back_sum[:, place] + found)

    def gin_store(g):
        place = pl.ds(g * GROUP, GROUP)
        return pltpu.make_async_copy(gin_ref.at[place], gin_hbm.at[0, place], store_sem.at[g])

    def gw_store(h):
        place = pl.ds(h * size, size)
        return pltpu.make_async_copy(
            gw_ref.at[place], gw_hbm.at[place], store_sem.at[groups + h]
        )

    def columns_back(g, back):
        back = jnp.concatenate(
            [back[:, i * lanes : (i + 1) * lanes] for i in range(GROUP)], axis=0
        )
        high, low = split(back)
        raster = jnp.dot(
            jnp.concatenate([high, low, high], axis=1),
            out_of[...],
            preferred_element_type=jnp.float32,
        )
        gin_ref[pl.ds(g * GROUP, GROUP)] = raster.reshape(GROUP, rows, cols).astype(
            jnp.bfloat16
        )
        gin_store(g).start()

    sum_and_mix(0)
    forward(1, 0)
    for t in range(1, dp):
        sp_arrival(t).wait_recv()
    for b in range(dp):
        rows_of(b)
    sum_and_mix(1)
    if nz > 2:
        forward(2, 0)
    pair_terms(me_d, 0)
    forward(1, 1)
    pair_terms(me_d, 1)
    terms(1, 0)
    if nz > 3:
        forward(3, 0)
    if nz > 2:
        forward(2, 1)
    l_rows_out.wait()
    rows_back(0)
    terms(1, 1)
    if nz > 2:
        terms(2, 0)
    l_out_of.wait()
    rows_back(1)
    if nz > 2:
        terms(2, 1)
    if nz > 3:
        terms(3, 0)
        forward(3, 1)
        terms(3, 1)
    for t in range(4, nz):
        for h in range(2):
            forward(t, h)
            terms(t, h)
    for h in range(2):
        gw_store(h).start()

    def leave(copy):
        copy.wait_send()

    for t in range(1, space):
        for piece in range(groups + 1):
            rs_copy(t, piece).wait_send()
        for h in range(2):
            ag_copy(t, h).wait_send()
    for t in range(1, dp):
        sp_copy(t).wait_send()
    for h in range(2):
        own_sends(h, leave)
        for t in range(1, nz):
            passed_on(t, h, leave, False)
    for g in range(groups):
        gin_store(g).wait()
    for h in range(2):
        gw_store(h).wait()


def fused_body(dp, space, cotangent, spectrum, weights):
    _, channels, rows, cols = cotangent.shape
    local, _, _, lanes = spectrum.shape
    modes = local * space
    own = channels // dp
    groups = channels // GROUP
    fixed = [jnp.asarray(t) for t in tables(modes, lanes // 2, rows, cols, space)]
    into, rows_in, rows_out, out_of = fixed
    f32 = jnp.float32
    dma = pltpu.SemaphoreType.DMA
    return pl.pallas_call(
        functools.partial(kernel, dp, space),
        out_shape=(
            jax.ShapeDtypeStruct(cotangent.shape, jnp.bfloat16),
            jax.ShapeDtypeStruct((local, own * channels, lanes), f32),
        ),
        in_specs=[pl.BlockSpec(memory_space=pl.ANY)] * 7,
        out_specs=[pl.BlockSpec(memory_space=pl.ANY)] * 2,
        scratch_shapes=[
            pltpu.VMEM((channels, rows, cols), jnp.bfloat16),
            pltpu.VMEM((local, own * channels, lanes), f32),
            pltpu.VMEM((channels, rows, cols), jnp.bfloat16),
            pltpu.VMEM((local, channels, lanes), f32),
            pltpu.VMEM(weights.shape, f32),
            pltpu.VMEM(into.shape, jnp.bfloat16),
            pltpu.VMEM(rows_in.shape[1:], jnp.bfloat16),
            pltpu.VMEM(rows_out.shape[1:], jnp.bfloat16),
            pltpu.VMEM(out_of.shape, jnp.bfloat16),
            pltpu.VMEM((modes, channels, lanes), f32),
            pltpu.VMEM((space - 1, local, channels, lanes), f32),
            pltpu.VMEM((dp, local, channels, lanes), f32),
            pltpu.VMEM((2, modes // 2, channels, lanes), f32),
            pltpu.VMEM((rows, channels * lanes), f32),
            pltpu.VMEM((dp, local * own, lanes), f32),
            pltpu.VMEM((dp, local * own, lanes), f32),
            pltpu.VMEM((dp, local * own, lanes), f32),
            pltpu.VMEM((dp, local * own, lanes), f32),
            dma((groups + 6,)),
            dma((groups + 2,)),
            dma((space - 1, groups + 1)),
            dma((space - 1, groups + 1)),
            dma((space - 1, 2)),
            dma((space - 1, 2)),
            dma((dp,)),
            dma((dp,)),
            dma((dp, 2)),
            dma((dp, 2)),
            dma((dp, 2)),
            dma((dp, 2)),
        ],
        compiler_params=pltpu.CompilerParams(
            collective_id=0, has_side_effects=True, vmem_limit_bytes=62 * 1024 * 1024
        ),
    )(cotangent, spectrum, weights, into, rows_in, rows_out, out_of)


def solution(mesh):
    placed = (
        P("dp", None, "space", None),
        P("space", "dp", None, None),
        P("space", None, None, None),
    )
    dp, space = mesh.shape["dp"], mesh.shape["space"]

    def body(cotangent, spectrum, weights):
        rasters, channels, rows, _ = cotangent.shape
        whole_rows = (
            rasters == 1
            and dp % 2 == 0
            and channels % dp == 0
            and channels % GROUP == 0
            and spectrum.shape[0] % 2 == 0
            and rows % 16 == 0
            and (spectrum.shape[0] * (channels // dp)) % 8 == 0
        )
        if whole_rows:
            return fused_body(dp, space, cotangent, spectrum, weights)
        return general_body(cotangent, spectrum, weights)

    return jax.shard_map(
        body,
        mesh=mesh,
        in_specs=placed,
        out_specs=(P("dp", None, "space", None), P("space", "dp", None)),
        check_vma=False,
    )
```

```python
import functools
import math

import jax
import jax.numpy as jnp
import ml_dtypes
import numpy as np
from jax import lax
from jax.experimental import pallas as pl
from jax.experimental.pallas import tpu as pltpu
from jax.sharding import PartitionSpec as P

MESH = pl.DeviceIdType.MESH
GROUP = 8


def column_basis(col_count, modes_y):
    position = jnp.arange(col_count, dtype=jnp.int32)
    frequency = jnp.arange(modes_y, dtype=jnp.int32)
    phase = position[:, None] * frequency[None, :] % col_count
    angles = phase.astype(jnp.float32) * (2.0 * math.pi / col_count)
    return jnp.concatenate([jnp.cos(angles), -jnp.sin(angles)], axis=1)


def row_basis(mode_count, first_row, row_count, height):
    frequency = jnp.arange(mode_count, dtype=jnp.int32)
    position = first_row + jnp.arange(row_count, dtype=jnp.int32)
    phase = frequency[:, None] * position[None, :] % height
    angles = phase.astype(jnp.float32) * (2.0 * math.pi / height)
    return (jnp.cos(angles), jnp.sin(angles))


def spectral_backward(spec_grad, weights, modes_y):
    hp = lax.Precision.HIGHEST
    grad_re, grad_im = (spec_grad[..., :modes_y], spec_grad[..., modes_y:])
    weight_re, weight_im = (weights[..., :modes_y], weights[..., modes_y:])
    real_part = jnp.einsum("kbox,kcox->kbcx", grad_re, weight_re, precision=hp) + jnp.einsum(
        "kbox,kcox->kbcx", grad_im, weight_im, precision=hp
    )
    imag_part = jnp.einsum("kbox,kcox->kbcx", grad_im, weight_re, precision=hp) - jnp.einsum(
        "kbox,kcox->kbcx", grad_re, weight_im, precision=hp
    )
    return jnp.concatenate([real_part, imag_part], axis=-1)


def weight_terms(spectrum, spec_grad, modes_y):
    hp = lax.Precision.HIGHEST
    spec_re, spec_im = (spectrum[..., :modes_y], spectrum[..., modes_y:])
    grad_re, grad_im = (spec_grad[..., :modes_y], spec_grad[..., modes_y:])
    real_part = jnp.einsum("kbcx,kbox->kcox", spec_re, grad_re, precision=hp) + jnp.einsum(
        "kbcx,kbox->kcox", spec_im, grad_im, precision=hp
    )
    imag_part = jnp.einsum("kbcx,kbox->kcox", spec_re, grad_im, precision=hp) - jnp.einsum(
        "kbcx,kbox->kcox", spec_im, grad_re, precision=hp
    )
    joined = jnp.concatenate([real_part, imag_part], axis=-1)
    return joined.reshape(joined.shape[0], joined.shape[1] * joined.shape[2], joined.shape[3])


def general_body(cotangent, spectrum, weights):
    hp = lax.Precision.HIGHEST
    space_count = lax.axis_size("space")
    raster_count, channels, row_count, col_count = cotangent.shape
    local_modes = spectrum.shape[0]
    modes_y = spectrum.shape[3] // 2
    height = row_count * space_count
    basis = column_basis(col_count, modes_y)
    first_row = lax.axis_index("space") * row_count
    col_spec = jnp.einsum(
        "rcxw,wj->rcxj", cotangent, basis, precision=hp, preferred_element_type=jnp.float32
    )
    forward_scale = 1.0 / math.sqrt(height * col_count)
    cosines, sines = row_basis(local_modes * lax.axis_size("space"), first_row, row_count, height)
    with_cos = jnp.einsum("kx,rcxj->krcj", cosines, col_spec, precision=hp)
    with_sin = jnp.einsum("kx,rcxj->krcj", sines, col_spec, precision=hp)
    joined = jnp.concatenate(
        [
            with_cos[..., :modes_y] + with_sin[..., modes_y:],
            with_cos[..., modes_y:] - with_sin[..., :modes_y],
        ],
        axis=-1,
    )
    spec_grad = lax.psum_scatter(joined * forward_scale, "space", scatter_dimension=0, tiled=True)
    input_spec = spectral_backward(spec_grad, weights, modes_y)
    local_terms = weight_terms(spectrum, spec_grad, modes_y)
    grad_weights = lax.psum_scatter(local_terms, "dp", scatter_dimension=1, tiled=True)
    shard_piece = lax.all_gather(input_spec, "space", axis=0, tiled=True)
    cosines, sines = row_basis(shard_piece.shape[0], first_row, row_count, height)
    back_cos = jnp.einsum("kx,krcj->rcxj", cosines, shard_piece, precision=hp)
    back_sin = jnp.einsum("kx,krcj->rcxj", sines, shard_piece, precision=hp)
    joined = jnp.concatenate(
        [
            back_cos[..., :modes_y] - back_sin[..., modes_y:],
            back_cos[..., modes_y:] + back_sin[..., :modes_y],
        ],
        axis=-1,
    )
    inverse_scale = 1.0 / math.sqrt(local_modes * space_count * modes_y)
    grad_input = (jnp.einsum("rcxj,wj->rcxw", joined, basis, precision=hp) * inverse_scale).astype(
        jnp.bfloat16
    )
    return (grad_input, grad_weights)


def halves(table):
    high = table.astype(ml_dtypes.bfloat16)
    low = (table - high.astype(np.float64)).astype(ml_dtypes.bfloat16)
    return high, low


def tables(modes, modes_y, rows, cols, space):
    height = rows * space
    angle = 2.0 * np.pi * (np.outer(np.arange(cols), np.arange(modes_y)) % cols) / cols
    high, low = halves(np.concatenate([np.cos(angle), -np.sin(angle)], axis=1))
    into = np.concatenate([high, low], axis=1)
    out_of = np.concatenate([high.T, high.T, low.T], axis=0)
    angle = 2.0 * np.pi * (np.outer(np.arange(modes), np.arange(height)) % height) / height
    cosines = np.cos(angle).reshape(modes, space, rows).transpose(1, 0, 2)
    sines = np.sin(angle).reshape(modes, space, rows).transpose(1, 0, 2)
    high, low = halves(np.concatenate([cosines, sines], axis=2) / math.sqrt(height * cols))
    rows_in = np.concatenate([high, low, high], axis=2)
    local = modes // space
    order = np.arange(modes).reshape(space, 2, local // 2).transpose(1, 0, 2).reshape(2, -1)
    both = np.concatenate([cosines[:, order], sines[:, order]], axis=2).transpose(0, 1, 3, 2)
    high, low = halves(both / math.sqrt(modes * modes_y))
    rows_out = np.concatenate([high, low, high], axis=3)
    return into, rows_in, rows_out, out_of


def split(values):
    high = values.astype(jnp.bfloat16)
    low = (values - high.astype(jnp.float32)).astype(jnp.bfloat16)
    return high, low


def kernel(
    dp, space,
    cot_hbm, spec_hbm, w_hbm, into_hbm, rows_in_hbm, rows_out_hbm, out_of_hbm,
    gin_hbm, gw_hbm,
    gin_ref, gw_ref, cot, spec, w, into, rows_in, rows_out, out_of,
    part, rs_in, gall, iall, back_sum, sp_out, sp_in, a_rows, b_rows,
    load_sem, store_sem, rs_send, rs_recv, ag_send, ag_recv, sp_send, sp_recv,
    up_send, down_send, sib_send, g_recv,
):
    me_d = lax.axis_index("dp")
    me_s = lax.axis_index("space")
    channels, rows, cols = cot.shape
    local = w.shape[0]
    modes = local * space
    lanes = w.shape[3]
    half = lanes // 2
    own = channels // dp
    groups = channels // GROUP

    def at(d, s):
        return {"dp": d, "space": s}

    def partner_d(t):
        return lax.rem(me_d + t, dp)

    def partner_s(t):
        return lax.rem(me_s + t, space)

    def source_s(t):
        return lax.rem(me_s + space - t, space)

    barrier = pltpu.get_barrier_semaphore()
    for t in range(1, dp):
        pl.semaphore_signal(barrier, inc=1, device_id=at(partner_d(t), me_s), device_id_type=MESH)
    for t in range(1, space):
        pl.semaphore_signal(barrier, inc=1, device_id=at(me_d, partner_s(t)), device_id_type=MESH)

    def load(n, src, dst):
        copy = pltpu.make_async_copy(src, dst, load_sem.at[n])
        copy.start()
        return copy

    l_into = load(0, into_hbm, into)
    l_cot = []
    for g in range(groups):
        place = pl.ds(g * GROUP, GROUP)
        l_cot.append(load(1 + g, cot_hbm.at[0, place], cot.at[place]))
    n = 1 + groups
    l_rows_in = load(n, rows_in_hbm.at[me_s], rows_in)
    l_spec = load(n + 1, spec_hbm.at[:, 0], spec)
    l_w = load(n + 2, w_hbm, w)
    l_rows_out = load(n + 3, rows_out_hbm.at[me_s], rows_out)
    l_out_of = load(n + 4, out_of_hbm, out_of)

    lane = lax.broadcasted_iota(jnp.int32, (1, lanes), 1)
    lower = lane < half
    sign = jnp.where(lower, 1.0, -1.0).astype(jnp.float32)

    def turn(values):
        return pltpu.roll(values, half, values.ndim - 1)

    size = local // 2

    def rs_copy(t, piece):
        there = partner_s(t)
        if piece < groups:
            first, place = 0, pl.ds(piece * GROUP, GROUP)
        else:
            first, place = size, pl.ds(0, channels)
        return pltpu.make_async_remote_copy(
            part.at[pl.ds(there * local + first, size), place],
            rs_in.at[t - 1, pl.ds(first, size), place],
            rs_send.at[t - 1, piece],
            rs_recv.at[t - 1, piece],
            device_id=at(me_d, there),
            device_id_type=MESH,
        )

    def sp_copy(t):
        there = partner_d(t)
        return pltpu.make_async_remote_copy(
            sp_out.at[there],
            sp_in.at[me_d],
            sp_send.at[t],
            sp_recv.at[t],
            device_id=at(there, me_s),
            device_id_type=MESH,
        )

    def sp_arrival(t):
        source = lax.rem(me_d + dp - t, dp)
        return pltpu.make_async_remote_copy(
            sp_out.at[source],
            sp_in.at[source],
            sp_send.at[t],
            sp_recv.at[t],
            device_id=at(source, me_s),
            device_id_type=MESH,
        )

    l_into.wait()
    l_rows_in.wait()
    for g in range(groups):
        l_cot[g].wait()
        block = cot[pl.ds(g * GROUP, GROUP)].reshape(GROUP * rows, cols)
        both = jnp.dot(block, into[...], preferred_element_type=jnp.float32)
        col = both[:, :lanes] + both[:, lanes:]
        turned = turn(col) * sign
        stacked = jnp.concatenate(
            [
                jnp.concatenate(
                    [col[i * rows : (i + 1) * rows], turned[i * rows : (i + 1) * rows]], axis=0
                )
                for i in range(GROUP)
            ],
            axis=1,
        )
        high, low = split(stacked)
        spectrum_part = jnp.dot(
            rows_in[...],
            jnp.concatenate([high, high, low], axis=0),
            preferred_element_type=jnp.float32,
        )
        for i in range(GROUP):
            part[:, g * GROUP + i, :] = spectrum_part[:, i * lanes : (i + 1) * lanes]
        if g == 0:
            pl.semaphore_wait(barrier, dp + space - 2)
        for t in range(1, space):
            rs_copy(t, g).start()
    for t in range(1, space):
        rs_copy(t, groups).start()

    l_spec.wait()
    for d in range(dp):
        for k in range(local):
            sp_out[d, k * own : (k + 1) * own, :] = spec[k, d * own : (d + 1) * own, :]
    for t in range(1, dp):
        sp_copy(t).start()
    sp_in[me_d] = sp_out[me_d]
    gw_ref[...] = jnp.zeros_like(gw_ref)

    z, core = me_d // 2, lax.rem(me_d, 2)
    nz = dp // 2
    twin = 1 - 2 * core

    def g_copy(b, h, there, sem):
        place = pl.ds(h * size, size)
        return pltpu.make_async_remote_copy(
            gall.at[b, place],
            gall.at[b, place],
            sem.at[b, h],
            g_recv.at[b, h],
            device_id=at(there, me_s),
            device_id_type=MESH,
        )

    def up(b, h):
        return g_copy(b, h, me_d + 2, up_send)

    def down(b, h):
        return g_copy(b, h, me_d - 2, down_send)

    def sibling(b, h):
        return g_copy(b, h, me_d + twin, sib_send)

    def own_sends(h, act):
        @pl.when(z < nz - 1)
        def _():
            act(up(me_d, h))

        @pl.when(z > 0)
        def _():
            act(down(me_d, h))

        act(sibling(me_d, h))

    def passed_on(t, h, act, arrive):
        @pl.when(z >= t)
        def _():
            below = me_d - 2 * t
            if arrive:
                down(below, h).wait_recv()

            @pl.when(z < nz - 1)
            def _():
                act(up(below, h))

            act(sibling(below, h))

        @pl.when(z + t < nz)
        def _():
            above = me_d + 2 * t
            if arrive:
                up(above, h).wait_recv()

            @pl.when(z > 0)
            def _():
                act(down(above, h))

            act(sibling(above, h))

    def forward(t, h):
        passed_on(t, h, lambda copy: copy.start(), True)

    def ag_copy(t, h):
        place = pl.ds(me_s * size, size)
        return pltpu.make_async_remote_copy(
            iall.at[h, place],
            iall.at[h, place],
            ag_send.at[t - 1, h],
            ag_recv.at[t - 1, h],
            device_id=at(me_d, partner_s(t)),
            device_id_type=MESH,
        )

    def ag_arrival(t, h):
        place = pl.ds(source_s(t) * size, size)
        return pltpu.make_async_remote_copy(
            iall.at[h, place],
            iall.at[h, place],
            ag_send.at[t - 1, h],
            ag_recv.at[t - 1, h],
            device_id=at(me_d, source_s(t)),
            device_id_type=MESH,
        )

    def sum_and_mix(h):
        for t in range(1, space):
            for piece in range(groups) if h == 0 else (groups,):
                rs_copy(t, piece).wait_recv()

        def gather_sum(k, carry):
            total = part[me_s * local + k]
            for t in range(1, space):
                total = total + rs_in[t - 1, k]
            gall[me_d, k] = total
            return carry

        lax.fori_loop(h * size, (h + 1) * size, gather_sum, 0, unroll=True)
        own_sends(h, lambda copy: copy.start())
        if h == 0:
            l_w.wait()

        def mix(k, carry):
            grad = gall[me_d, k]
            weight = w[k]
            plain = jnp.sum(weight * grad[None], axis=1)
            cross = jnp.sum(weight * turn(grad)[None], axis=1)
            mixed = jnp.where(lower, plain + turn(plain), turn(cross) - cross)
            iall[h, me_s * size + k - h * size] = mixed
            return carry

        lax.fori_loop(h * size, (h + 1) * size, mix, 0, unroll=True)
        for t in range(1, space):
            ag_copy(t, h).start()

    def rows_of(b):
        saved = sp_in[b]
        a_rows[b] = jnp.where(lower, saved, turn(saved))
        b_rows[b] = jnp.where(lower, turn(saved), -saved)

    def add_terms(blocks, h):
        def one(k, carry):
            grads = [gall[b, k] for b in blocks]
            turned = [turn(grad) for grad in grads]
            for c in range(own):
                row = pl.ds(k * own + c, 1)
                place = pl.ds(c * channels, channels)
                total = gw_ref[k, place, :]
                for b, grad, other in zip(blocks, grads, turned):
                    total = total + (a_rows[b, row, :] * grad + b_rows[b, row, :] * other)
                gw_ref[k, place, :] = total
            return carry

        lax.fori_loop(h * size, (h + 1) * size, one, 0, unroll=True)

    def pair_terms(b, h):
        sibling(b + twin, h).wait_recv()
        add_terms((b, b + twin), h)

    def terms(t, h):
        @pl.when(z >= t)
        def _():
            pair_terms(me_d - 2 * t, h)

        @pl.when(z + t < nz)
        def _():
            pair_terms(me_d + 2 * t, h)

    def rows_back(h):
        for t in range(1, space):
            ag_arrival(t, h).wait_recv()
        for g in range(groups):
            mixed = jnp.concatenate([iall[h, :, g * GROUP + i, :] for i in range(GROUP)], axis=1)
            turned = jnp.concatenate(
                [-sign * turn(mixed[:, i * lanes : (i + 1) * lanes]) for i in range(GROUP)],
                axis=1,
            )
            high, low = split(jnp.concatenate([mixed, turned], axis=0))
            found = jnp.dot(
                rows_out[h],
                jnp.concatenate([high, high, low], axis=0),
                preferred_element_type=jnp.float32,
            )
            place = pl.ds(g * GROUP * lanes, GROUP * lanes)
            if h == 0:
                back_sum[:, place] = found
            else:
                columns_back(g, back_sum[:, place] + found)

    def gin_store(g):
        place = pl.ds(g * GROUP, GROUP)
        return pltpu.make_async_copy(gin_ref.at[place], gin_hbm.at[0, place], store_sem.at[g])

    def gw_store(h):
        place = pl.ds(h * size, size)
        return pltpu.make_async_copy(
            gw_ref.at[place], gw_hbm.at[place], store_sem.at[groups + h]
        )

    def columns_back(g, back):
        back = jnp.concatenate(
            [back[:, i * lanes : (i + 1) * lanes] for i in range(GROUP)], axis=0
        )
        high, low = split(back)
        raster = jnp.dot(
            jnp.concatenate([high, low, high], axis=1),
            out_of[...],
            preferred_element_type=jnp.float32,
        )
        gin_ref[pl.ds(g * GROUP, GROUP)] = raster.reshape(GROUP, rows, cols).astype(
            jnp.bfloat16
        )
        gin_store(g).start()

    sum_and_mix(0)
    forward(1, 0)
    for t in range(1, dp):
        sp_arrival(t).wait_recv()
    for b in range(dp):
        rows_of(b)
    sum_and_mix(1)
    if nz > 2:
        forward(2, 0)
    pair_terms(me_d, 0)
    forward(1, 1)
    pair_terms(me_d, 1)
    terms(1, 0)
    if nz > 3:
        forward(3, 0)
    if nz > 2:
        forward(2, 1)
    l_rows_out.wait()
    rows_back(0)
    terms(1, 1)
    if nz > 2:
        terms(2, 0)
    l_out_of.wait()
    rows_back(1)
    if nz > 2:
        terms(2, 1)
    if nz > 3:
        terms(3, 0)
        forward(3, 1)
        terms(3, 1)
    for t in range(4, nz):
        for h in range(2):
            forward(t, h)
            terms(t, h)
    for h in range(2):
        gw_store(h).start()

    def leave(copy):
        copy.wait_send()

    for t in range(1, space):
        for piece in range(groups + 1):
            rs_copy(t, piece).wait_send()
        for h in range(2):
            ag_copy(t, h).wait_send()
    for t in range(1, dp):
        sp_copy(t).wait_send()
    for h in range(2):
        own_sends(h, leave)
        for t in range(1, nz):
            passed_on(t, h, leave, False)
    for g in range(groups):
        gin_store(g).wait()
    for h in range(2):
        gw_store(h).wait()


def fused_body(dp, space, cotangent, spectrum, weights):
    _, channels, rows, cols = cotangent.shape
    local, _, _, lanes = spectrum.shape
    modes = local * space
    own = channels // dp
    groups = channels // GROUP
    fixed = [jnp.asarray(t) for t in tables(modes, lanes // 2, rows, cols, space)]
    into, rows_in, rows_out, out_of = fixed
    f32 = jnp.float32
    dma = pltpu.SemaphoreType.DMA
    return pl.pallas_call(
        functools.partial(kernel, dp, space),
        out_shape=(
            jax.ShapeDtypeStruct(cotangent.shape, jnp.bfloat16),
            jax.ShapeDtypeStruct((local, own * channels, lanes), f32),
        ),
        in_specs=[pl.BlockSpec(memory_space=pl.ANY)] * 7,
        out_specs=[pl.BlockSpec(memory_space=pl.ANY)] * 2,
        scratch_shapes=[
            pltpu.VMEM((channels, rows, cols), jnp.bfloat16),
            pltpu.VMEM((local, own * channels, lanes), f32),
            pltpu.VMEM((channels, rows, cols), jnp.bfloat16),
            pltpu.VMEM((local, channels, lanes), f32),
            pltpu.VMEM(weights.shape, f32),
            pltpu.VMEM(into.shape, jnp.bfloat16),
            pltpu.VMEM(rows_in.shape[1:], jnp.bfloat16),
            pltpu.VMEM(rows_out.shape[1:], jnp.bfloat16),
            pltpu.VMEM(out_of.shape, jnp.bfloat16),
            pltpu.VMEM((modes, channels, lanes), f32),
            pltpu.VMEM((space - 1, local, channels, lanes), f32),
            pltpu.VMEM((dp, local, channels, lanes), f32),
            pltpu.VMEM((2, modes // 2, channels, lanes), f32),
            pltpu.VMEM((rows, channels * lanes), f32),
            pltpu.VMEM((dp, local * own, lanes), f32),
            pltpu.VMEM((dp, local * own, lanes), f32),
            pltpu.VMEM((dp, local * own, lanes), f32),
            pltpu.VMEM((dp, local * own, lanes), f32),
            dma((groups + 6,)),
            dma((groups + 2,)),
            dma((space - 1, groups + 1)),
            dma((space - 1, groups + 1)),
            dma((space - 1, 2)),
            dma((space - 1, 2)),
            dma((dp,)),
            dma((dp,)),
            dma((dp, 2)),
            dma((dp, 2)),
            dma((dp, 2)),
            dma((dp, 2)),
        ],
        compiler_params=pltpu.CompilerParams(
            collective_id=0, has_side_effects=True, vmem_limit_bytes=62 * 1024 * 1024
        ),
    )(cotangent, spectrum, weights, into, rows_in, rows_out, out_of)


def solution(mesh):
    placed = (
        P("dp", None, "space", None),
        P("space", "dp", None, None),
        P("space", None, None, None),
    )
    dp, space = mesh.shape["dp"], mesh.shape["space"]

    def body(cotangent, spectrum, weights):
        rasters, channels, rows, _ = cotangent.shape
        whole_rows = (
            rasters == 1
            and dp % 2 == 0
            and channels % dp == 0
            and channels % GROUP == 0
            and spectrum.shape[0] % 2 == 0
            and rows % 16 == 0
            and (spectrum.shape[0] * (channels // dp)) % 8 == 0
        )
        if whole_rows:
            return fused_body(dp, space, cotangent, spectrum, weights)
        return general_body(cotangent, spectrum, weights)

    return jax.shard_map(
        body,
        mesh=mesh,
        in_specs=placed,
        out_specs=(P("dp", None, "space", None), P("space", "dp", None)),
        check_vma=False,
    )
```

```python
import functools
import math

import jax
import jax.numpy as jnp
import ml_dtypes
import numpy as np
from jax import lax
from jax.experimental import pallas as pl
from jax.experimental.pallas import tpu as pltpu
from jax.sharding import PartitionSpec as P

MESH = pl.DeviceIdType.MESH
GROUP = 8


def column_basis(col_count, modes_y):
    position = jnp.arange(col_count, dtype=jnp.int32)
    frequency = jnp.arange(modes_y, dtype=jnp.int32)
    phase = position[:, None] * frequency[None, :] % col_count
    angles = phase.astype(jnp.float32) * (2.0 * math.pi / col_count)
    return jnp.concatenate([jnp.cos(angles), -jnp.sin(angles)], axis=1)


def row_basis(mode_count, first_row, row_count, height):
    frequency = jnp.arange(mode_count, dtype=jnp.int32)
    position = first_row + jnp.arange(row_count, dtype=jnp.int32)
    phase = frequency[:, None] * position[None, :] % height
    angles = phase.astype(jnp.float32) * (2.0 * math.pi / height)
    return (jnp.cos(angles), jnp.sin(angles))


def spectral_backward(spec_grad, weights, modes_y):
    hp = lax.Precision.HIGHEST
    grad_re, grad_im = (spec_grad[..., :modes_y], spec_grad[..., modes_y:])
    weight_re, weight_im = (weights[..., :modes_y], weights[..., modes_y:])
    real_part = jnp.einsum("kbox,kcox->kbcx", grad_re, weight_re, precision=hp) + jnp.einsum(
        "kbox,kcox->kbcx", grad_im, weight_im, precision=hp
    )
    imag_part = jnp.einsum("kbox,kcox->kbcx", grad_im, weight_re, precision=hp) - jnp.einsum(
        "kbox,kcox->kbcx", grad_re, weight_im, precision=hp
    )
    return jnp.concatenate([real_part, imag_part], axis=-1)


def weight_terms(spectrum, spec_grad, modes_y):
    hp = lax.Precision.HIGHEST
    spec_re, spec_im = (spectrum[..., :modes_y], spectrum[..., modes_y:])
    grad_re, grad_im = (spec_grad[..., :modes_y], spec_grad[..., modes_y:])
    real_part = jnp.einsum("kbcx,kbox->kcox", spec_re, grad_re, precision=hp) + jnp.einsum(
        "kbcx,kbox->kcox", spec_im, grad_im, precision=hp
    )
    imag_part = jnp.einsum("kbcx,kbox->kcox", spec_re, grad_im, precision=hp) - jnp.einsum(
        "kbcx,kbox->kcox", spec_im, grad_re, precision=hp
    )
    joined = jnp.concatenate([real_part, imag_part], axis=-1)
    return joined.reshape(joined.shape[0], joined.shape[1] * joined.shape[2], joined.shape[3])


def general_body(cotangent, spectrum, weights):
    hp = lax.Precision.HIGHEST
    space_count = lax.axis_size("space")
    raster_count, channels, row_count, col_count = cotangent.shape
    local_modes = spectrum.shape[0]
    modes_y = spectrum.shape[3] // 2
    height = row_count * space_count
    basis = column_basis(col_count, modes_y)
    first_row = lax.axis_index("space") * row_count
    col_spec = jnp.einsum(
        "rcxw,wj->rcxj", cotangent, basis, precision=hp, preferred_element_type=jnp.float32
    )
    forward_scale = 1.0 / math.sqrt(height * col_count)
    cosines, sines = row_basis(local_modes * lax.axis_size("space"), first_row, row_count, height)
    with_cos = jnp.einsum("kx,rcxj->krcj", cosines, col_spec, precision=hp)
    with_sin = jnp.einsum("kx,rcxj->krcj", sines, col_spec, precision=hp)
    joined = jnp.concatenate(
        [
            with_cos[..., :modes_y] + with_sin[..., modes_y:],
            with_cos[..., modes_y:] - with_sin[..., :modes_y],
        ],
        axis=-1,
    )
    spec_grad = lax.psum_scatter(joined * forward_scale, "space", scatter_dimension=0, tiled=True)
    input_spec = spectral_backward(spec_grad, weights, modes_y)
    local_terms = weight_terms(spectrum, spec_grad, modes_y)
    grad_weights = lax.psum_scatter(local_terms, "dp", scatter_dimension=1, tiled=True)
    shard_piece = lax.all_gather(input_spec, "space", axis=0, tiled=True)
    cosines, sines = row_basis(shard_piece.shape[0], first_row, row_count, height)
    back_cos = jnp.einsum("kx,krcj->rcxj", cosines, shard_piece, precision=hp)
    back_sin = jnp.einsum("kx,krcj->rcxj", sines, shard_piece, precision=hp)
    joined = jnp.concatenate(
        [
            back_cos[..., :modes_y] - back_sin[..., modes_y:],
            back_cos[..., modes_y:] + back_sin[..., :modes_y],
        ],
        axis=-1,
    )
    inverse_scale = 1.0 / math.sqrt(local_modes * space_count * modes_y)
    grad_input = (jnp.einsum("rcxj,wj->rcxw", joined, basis, precision=hp) * inverse_scale).astype(
        jnp.bfloat16
    )
    return (grad_input, grad_weights)


def halves(table):
    high = table.astype(ml_dtypes.bfloat16)
    low = (table - high.astype(np.float64)).astype(ml_dtypes.bfloat16)
    return high, low


def tables(modes, modes_y, rows, cols, space):
    height = rows * space
    angle = 2.0 * np.pi * (np.outer(np.arange(cols), np.arange(modes_y)) % cols) / cols
    high, low = halves(np.concatenate([np.cos(angle), -np.sin(angle)], axis=1))
    into = np.concatenate([high, low], axis=1)
    out_of = np.concatenate([high.T, high.T, low.T], axis=0)
    angle = 2.0 * np.pi * (np.outer(np.arange(modes), np.arange(height)) % height) / height
    cosines = np.cos(angle).reshape(modes, space, rows).transpose(1, 0, 2)
    sines = np.sin(angle).reshape(modes, space, rows).transpose(1, 0, 2)
    high, low = halves(np.concatenate([cosines, sines], axis=2) / math.sqrt(height * cols))
    rows_in = np.concatenate([high, low, high], axis=2)
    local = modes // space
    order = np.arange(modes).reshape(space, 2, local // 2).transpose(1, 0, 2).reshape(2, -1)
    both = np.concatenate([cosines[:, order], sines[:, order]], axis=2).transpose(0, 1, 3, 2)
    high, low = halves(both / math.sqrt(modes * modes_y))
    rows_out = np.concatenate([high, low, high], axis=3)
    return into, rows_in, rows_out, out_of


def split(values):
    high = values.astype(jnp.bfloat16)
    low = (values - high.astype(jnp.float32)).astype(jnp.bfloat16)
    return high, low


def kernel(
    dp, space,
    cot_hbm, spec_hbm, w_hbm, into_hbm, rows_in_hbm, rows_out_hbm,
    back_hbm, gw_hbm,
    back_ref, gw_ref, cot, spec, w, into, rows_in, rows_out,
    part, rs_in, gall, iall, back_sum, sp_out, sp_in, a_rows, b_rows,
    load_sem, store_sem, rs_send, rs_recv, ag_send, ag_recv, sp_send, sp_recv,
    up_send, down_send, sib_send, g_recv,
):
    me_d = lax.axis_index("dp")
    me_s = lax.axis_index("space")
    channels, rows, cols = cot.shape
    local = w.shape[0]
    modes = local * space
    lanes = w.shape[3]
    half = lanes // 2
    own = channels // dp
    groups = channels // GROUP

    def at(d, s):
        return {"dp": d, "space": s}

    def partner_d(t):
        return lax.rem(me_d + t, dp)

    def partner_s(t):
        return lax.rem(me_s + t, space)

    def source_s(t):
        return lax.rem(me_s + space - t, space)

    barrier = pltpu.get_barrier_semaphore()
    for t in range(1, dp):
        pl.semaphore_signal(barrier, inc=1, device_id=at(partner_d(t), me_s), device_id_type=MESH)
    for t in range(1, space):
        pl.semaphore_signal(barrier, inc=1, device_id=at(me_d, partner_s(t)), device_id_type=MESH)

    def load(n, src, dst):
        copy = pltpu.make_async_copy(src, dst, load_sem.at[n])
        copy.start()
        return copy

    l_into = load(0, into_hbm, into)
    l_cot = []
    for g in range(groups):
        place = pl.ds(g * GROUP, GROUP)
        l_cot.append(load(1 + g, cot_hbm.at[0, place], cot.at[place]))
    n = 1 + groups
    l_rows_in = load(n, rows_in_hbm.at[me_s], rows_in)
    l_spec = load(n + 1, spec_hbm.at[:, 0], spec)
    l_w = load(n + 2, w_hbm, w)
    l_rows_out = load(n + 3, rows_out_hbm.at[me_s], rows_out)

    lane = lax.broadcasted_iota(jnp.int32, (1, lanes), 1)
    lower = lane < half
    sign = jnp.where(lower, 1.0, -1.0).astype(jnp.float32)

    def turn(values):
        return pltpu.roll(values, half, values.ndim - 1)

    size = local // 2

    def rs_copy(t, piece):
        there = partner_s(t)
        if piece < groups:
            first, place = 0, pl.ds(piece * GROUP, GROUP)
        else:
            first, place = size, pl.ds(0, channels)
        return pltpu.make_async_remote_copy(
            part.at[pl.ds(there * local + first, size), place],
            rs_in.at[t - 1, pl.ds(first, size), place],
            rs_send.at[t - 1, piece],
            rs_recv.at[t - 1, piece],
            device_id=at(me_d, there),
            device_id_type=MESH,
        )

    def sp_copy(t):
        there = partner_d(t)
        return pltpu.make_async_remote_copy(
            sp_out.at[there],
            sp_in.at[me_d],
            sp_send.at[t],
            sp_recv.at[t],
            device_id=at(there, me_s),
            device_id_type=MESH,
        )

    def sp_arrival(t):
        source = lax.rem(me_d + dp - t, dp)
        return pltpu.make_async_remote_copy(
            sp_out.at[source],
            sp_in.at[source],
            sp_send.at[t],
            sp_recv.at[t],
            device_id=at(source, me_s),
            device_id_type=MESH,
        )

    l_into.wait()
    l_rows_in.wait()
    for g in range(groups):
        l_cot[g].wait()
        block = cot[pl.ds(g * GROUP, GROUP)].reshape(GROUP * rows, cols)
        both = jnp.dot(block, into[...], preferred_element_type=jnp.float32)
        col = both[:, :lanes] + both[:, lanes:]
        turned = turn(col) * sign
        stacked = jnp.concatenate(
            [
                jnp.concatenate(
                    [col[i * rows : (i + 1) * rows], turned[i * rows : (i + 1) * rows]], axis=0
                )
                for i in range(GROUP)
            ],
            axis=1,
        )
        high, low = split(stacked)
        spectrum_part = jnp.dot(
            rows_in[...],
            jnp.concatenate([high, high, low], axis=0),
            preferred_element_type=jnp.float32,
        )
        for i in range(GROUP):
            part[:, g * GROUP + i, :] = spectrum_part[:, i * lanes : (i + 1) * lanes]
        if g == 0:
            pl.semaphore_wait(barrier, dp + space - 2)
        for t in range(1, space):
            rs_copy(t, g).start()
    for t in range(1, space):
        rs_copy(t, groups).start()

    l_spec.wait()
    for d in range(dp):
        for k in range(local):
            sp_out[d, k * own : (k + 1) * own, :] = spec[k, d * own : (d + 1) * own, :]
    for t in range(1, dp):
        sp_copy(t).start()
    sp_in[me_d] = sp_out[me_d]
    gw_ref[...] = jnp.zeros_like(gw_ref)

    z, core = me_d // 2, lax.rem(me_d, 2)
    nz = dp // 2
    twin = 1 - 2 * core

    def g_copy(b, h, there, sem):
        place = pl.ds(h * size, size)
        return pltpu.make_async_remote_copy(
            gall.at[b, place],
            gall.at[b, place],
            sem.at[b, h],
            g_recv.at[b, h],
            device_id=at(there, me_s),
            device_id_type=MESH,
        )

    def up(b, h):
        return g_copy(b, h, me_d + 2, up_send)

    def down(b, h):
        return g_copy(b, h, me_d - 2, down_send)

    def sibling(b, h):
        return g_copy(b, h, me_d + twin, sib_send)

    def own_sends(h, act):
        @pl.when(z < nz - 1)
        def _():
            act(up(me_d, h))

        @pl.when(z > 0)
        def _():
            act(down(me_d, h))

        act(sibling(me_d, h))

    def passed_on(t, h, act, arrive):
        @pl.when(z >= t)
        def _():
            below = me_d - 2 * t
            if arrive:
                down(below, h).wait_recv()

            @pl.when(z < nz - 1)
            def _():
                act(up(below, h))

            act(sibling(below, h))

        @pl.when(z + t < nz)
        def _():
            above = me_d + 2 * t
            if arrive:
                up(above, h).wait_recv()

            @pl.when(z > 0)
            def _():
                act(down(above, h))

            act(sibling(above, h))

    def forward(t, h):
        passed_on(t, h, lambda copy: copy.start(), True)

    def ag_copy(t, h):
        place = pl.ds(me_s * size, size)
        return pltpu.make_async_remote_copy(
            iall.at[h, place],
            iall.at[h, place],
            ag_send.at[t - 1, h],
            ag_recv.at[t - 1, h],
            device_id=at(me_d, partner_s(t)),
            device_id_type=MESH,
        )

    def ag_arrival(t, h):
        place = pl.ds(source_s(t) * size, size)
        return pltpu.make_async_remote_copy(
            iall.at[h, place],
            iall.at[h, place],
            ag_send.at[t - 1, h],
            ag_recv.at[t - 1, h],
            device_id=at(me_d, source_s(t)),
            device_id_type=MESH,
        )

    def summed(h):
        def gather_sum(k, carry):
            total = part[me_s * local + k]
            for t in range(1, space):
                total = total + rs_in[t - 1, k]
            gall[me_d, k] = total
            return carry

        lax.fori_loop(h * size, (h + 1) * size, gather_sum, 0, unroll=True)
        own_sends(h, lambda copy: copy.start())

    def mixed_by(h):
        def mix(k, carry):
            grad = gall[me_d, k]
            weight = w[k]
            plain = jnp.sum(weight * grad[None], axis=1)
            cross = jnp.sum(weight * turn(grad)[None], axis=1)
            mixed = jnp.where(lower, plain + turn(plain), turn(cross) - cross)
            iall[h, me_s * size + k - h * size] = mixed
            return carry

        lax.fori_loop(h * size, (h + 1) * size, mix, 0, unroll=True)

    def ag_start(h):
        for t in range(1, space):
            ag_copy(t, h).start()

    def rows_of(b):
        saved = sp_in[b]
        a_rows[b] = jnp.where(lower, saved, turn(saved))
        b_rows[b] = jnp.where(lower, turn(saved), -saved)

    def add_terms(blocks, h):
        def one(k, carry):
            grads = [gall[b, k] for b in blocks]
            turned = [turn(grad) for grad in grads]
            for c in range(own):
                row = pl.ds(k * own + c, 1)
                place = pl.ds(c * channels, channels)
                total = gw_ref[k, place, :]
                for b, grad, other in zip(blocks, grads, turned):
                    total = total + (a_rows[b, row, :] * grad + b_rows[b, row, :] * other)
                gw_ref[k, place, :] = total
            return carry

        lax.fori_loop(h * size, (h + 1) * size, one, 0, unroll=True)

    def pair_terms(b, h):
        sibling(b + twin, h).wait_recv()
        add_terms((b, b + twin), h)

    def terms(t, h):
        @pl.when(z >= t)
        def _():
            pair_terms(me_d - 2 * t, h)

        @pl.when(z + t < nz)
        def _():
            pair_terms(me_d + 2 * t, h)

    def rows_back(h):
        for t in range(1, space):
            ag_arrival(t, h).wait_recv()
        for g in range(groups):
            mixed = jnp.concatenate([iall[h, :, g * GROUP + i, :] for i in range(GROUP)], axis=1)
            turned = jnp.concatenate(
                [-sign * turn(mixed[:, i * lanes : (i + 1) * lanes]) for i in range(GROUP)],
                axis=1,
            )
            high, low = split(jnp.concatenate([mixed, turned], axis=0))
            found = jnp.dot(
                rows_out[h],
                jnp.concatenate([high, high, low], axis=0),
                preferred_element_type=jnp.float32,
            )
            place = pl.ds(g * GROUP * lanes, GROUP * lanes)
            if h == 0:
                back_sum[:, place] = found
            else:
                found = back_sum[:, place] + found
                high, low = split(
                    jnp.concatenate(
                        [found[:, i * lanes : (i + 1) * lanes] for i in range(GROUP)], axis=0
                    )
                )
                place = pl.ds(g * GROUP * rows, GROUP * rows)
                back_ref[place, pl.ds(0, lanes)] = high
                back_ref[place, pl.ds(lanes, lanes)] = low
                back_store(g).start()

    def back_store(g):
        place = pl.ds(g * GROUP * rows, GROUP * rows)
        return pltpu.make_async_copy(back_ref.at[place], back_hbm.at[place], store_sem.at[g])

    def gw_store(h):
        place = pl.ds(h * size, size)
        return pltpu.make_async_copy(
            gw_ref.at[place], gw_hbm.at[place], store_sem.at[groups + h]
        )

    for t in range(1, space):
        for piece in range(groups):
            rs_copy(t, piece).wait_recv()
    summed(0)
    l_w.wait()
    mixed_by(0)
    forward(1, 0)
    for t in range(1, dp):
        sp_arrival(t).wait_recv()
    for b in range(dp):
        rows_of(b)
    for t in range(1, space):
        rs_copy(t, groups).wait_recv()
    ag_start(0)
    summed(1)
    mixed_by(1)
    ag_start(1)
    if nz > 2:
        forward(2, 0)
    pair_terms(me_d, 0)
    pair_terms(me_d, 1)
    forward(1, 1)
    terms(1, 0)
    if nz > 3:
        forward(3, 0)
    if nz > 2:
        forward(2, 1)
    l_rows_out.wait()
    rows_back(0)
    terms(1, 1)
    if nz > 2:
        terms(2, 0)
    if nz > 3:
        terms(3, 0)
        forward(3, 1)
    rows_back(1)
    if nz > 2:
        terms(2, 1)
    if nz > 3:
        terms(3, 1)
    for t in range(4, nz):
        for h in range(2):
            forward(t, h)
            terms(t, h)
    for h in range(2):
        gw_store(h).start()

    def leave(copy):
        copy.wait_send()

    for t in range(1, space):
        for piece in range(groups + 1):
            rs_copy(t, piece).wait_send()
        for h in range(2):
            ag_copy(t, h).wait_send()
    for t in range(1, dp):
        sp_copy(t).wait_send()
    for h in range(2):
        own_sends(h, leave)
        for t in range(1, nz):
            passed_on(t, h, leave, False)
    for g in range(groups):
        back_store(g).wait()
    for h in range(2):
        gw_store(h).wait()


def columns_kernel(
    back_hbm, terms_hbm, out_of_hbm, gin_hbm, gw_hbm,
    back, terms, out_of, gin, load_sem, store_sem,
):
    channels, rows, cols = gin.shape
    groups = channels // GROUP
    lanes = back.shape[1] // 2
    count = GROUP * rows
    l_out_of = pltpu.make_async_copy(out_of_hbm, out_of, load_sem.at[groups])
    l_out_of.start()
    loads, stores = [], []
    for g in range(groups):
        place = pl.ds(g * count, count)
        loads.append(pltpu.make_async_copy(back_hbm.at[place], back.at[place], load_sem.at[g]))
        loads[g].start()
    l_terms = pltpu.make_async_copy(terms_hbm, terms, load_sem.at[groups + 1])
    l_terms.start()
    l_out_of.wait()
    for g in range(groups):
        loads[g].wait()
        both = back[pl.ds(g * count, count)]
        raster = jnp.dot(
            jnp.concatenate([both, both[:, :lanes]], axis=1),
            out_of[...],
            preferred_element_type=jnp.float32,
        )
        place = pl.ds(g * GROUP, GROUP)
        gin[place] = raster.reshape(GROUP, rows, cols).astype(jnp.bfloat16)
        stores.append(pltpu.make_async_copy(gin.at[place], gin_hbm.at[0, place], store_sem.at[g]))
        stores[g].start()
        if g == 0:
            l_terms.wait()
            s_terms = pltpu.make_async_copy(terms, gw_hbm, store_sem.at[groups])
            s_terms.start()
    for store in stores:
        store.wait()
    s_terms.wait()


def fused_body(dp, space, cotangent, spectrum, weights):
    _, channels, rows, cols = cotangent.shape
    local, _, _, lanes = spectrum.shape
    modes = local * space
    own = channels // dp
    groups = channels // GROUP
    fixed = [jnp.asarray(t) for t in tables(modes, lanes // 2, rows, cols, space)]
    into, rows_in, rows_out, out_of = fixed
    f32 = jnp.float32
    dma = pltpu.SemaphoreType.DMA
    back, terms = pl.pallas_call(
        functools.partial(kernel, dp, space),
        out_shape=(
            jax.ShapeDtypeStruct((channels * rows, 2 * lanes), jnp.bfloat16),
            jax.ShapeDtypeStruct((local, own * channels, lanes), f32),
        ),
        in_specs=[pl.BlockSpec(memory_space=pl.ANY)] * 6,
        out_specs=[pl.BlockSpec(memory_space=pl.ANY)] * 2,
        scratch_shapes=[
            pltpu.VMEM((channels * rows, 2 * lanes), jnp.bfloat16),
            pltpu.VMEM((local, own * channels, lanes), f32),
            pltpu.VMEM((channels, rows, cols), jnp.bfloat16),
            pltpu.VMEM((local, channels, lanes), f32),
            pltpu.VMEM(weights.shape, f32),
            pltpu.VMEM(into.shape, jnp.bfloat16),
            pltpu.VMEM(rows_in.shape[1:], jnp.bfloat16),
            pltpu.VMEM(rows_out.shape[1:], jnp.bfloat16),
            pltpu.VMEM((modes, channels, lanes), f32),
            pltpu.VMEM((space - 1, local, channels, lanes), f32),
            pltpu.VMEM((dp, local, channels, lanes), f32),
            pltpu.VMEM((2, modes // 2, channels, lanes), f32),
            pltpu.VMEM((rows, channels * lanes), f32),
            pltpu.VMEM((dp, local * own, lanes), f32),
            pltpu.VMEM((dp, local * own, lanes), f32),
            pltpu.VMEM((dp, local * own, lanes), f32),
            pltpu.VMEM((dp, local * own, lanes), f32),
            dma((groups + 5,)),
            dma((groups + 2,)),
            dma((space - 1, groups + 1)),
            dma((space - 1, groups + 1)),
            dma((space - 1, 2)),
            dma((space - 1, 2)),
            dma((dp,)),
            dma((dp,)),
            dma((dp, 2)),
            dma((dp, 2)),
            dma((dp, 2)),
            dma((dp, 2)),
        ],
        compiler_params=pltpu.CompilerParams(
            collective_id=0, has_side_effects=True, vmem_limit_bytes=62 * 1024 * 1024
        ),
    )(cotangent, spectrum, weights, into, rows_in, rows_out)
    return pl.pallas_call(
        columns_kernel,
        out_shape=(
            jax.ShapeDtypeStruct(cotangent.shape, jnp.bfloat16),
            jax.ShapeDtypeStruct(terms.shape, f32),
        ),
        in_specs=[pl.BlockSpec(memory_space=pl.ANY)] * 3,
        out_specs=[pl.BlockSpec(memory_space=pl.ANY)] * 2,
        scratch_shapes=[
            pltpu.VMEM(back.shape, jnp.bfloat16),
            pltpu.VMEM(terms.shape, f32),
            pltpu.VMEM(out_of.shape, jnp.bfloat16),
            pltpu.VMEM(cotangent.shape[1:], jnp.bfloat16),
            dma((groups + 2,)),
            dma((groups + 1,)),
        ],
        compiler_params=pltpu.CompilerParams(vmem_limit_bytes=62 * 1024 * 1024),
    )(back, terms, out_of)


def solution(mesh):
    placed = (
        P("dp", None, "space", None),
        P("space", "dp", None, None),
        P("space", None, None, None),
    )
    dp, space = mesh.shape["dp"], mesh.shape["space"]

    def body(cotangent, spectrum, weights):
        rasters, channels, rows, _ = cotangent.shape
        whole_rows = (
            rasters == 1
            and dp % 2 == 0
            and channels % dp == 0
            and channels % GROUP == 0
            and spectrum.shape[0] % 2 == 0
            and rows % 16 == 0
            and (spectrum.shape[0] * (channels // dp)) % 8 == 0
        )
        if whole_rows:
            return fused_body(dp, space, cotangent, spectrum, weights)
        return general_body(cotangent, spectrum, weights)

    return jax.shard_map(
        body,
        mesh=mesh,
        in_specs=placed,
        out_specs=(P("dp", None, "space", None), P("space", "dp", None)),
        check_vma=False,
    )
```

```python
import functools
import math

import jax
import jax.numpy as jnp
import ml_dtypes
import numpy as np
from jax import lax
from jax.experimental import pallas as pl
from jax.experimental.pallas import tpu as pltpu
from jax.sharding import PartitionSpec as P

MESH = pl.DeviceIdType.MESH
GROUP = 8
COLUMNS = 4
PARTS = 4


def column_basis(col_count, modes_y):
    position = jnp.arange(col_count, dtype=jnp.int32)
    frequency = jnp.arange(modes_y, dtype=jnp.int32)
    phase = position[:, None] * frequency[None, :] % col_count
    angles = phase.astype(jnp.float32) * (2.0 * math.pi / col_count)
    return jnp.concatenate([jnp.cos(angles), -jnp.sin(angles)], axis=1)


def row_basis(mode_count, first_row, row_count, height):
    frequency = jnp.arange(mode_count, dtype=jnp.int32)
    position = first_row + jnp.arange(row_count, dtype=jnp.int32)
    phase = frequency[:, None] * position[None, :] % height
    angles = phase.astype(jnp.float32) * (2.0 * math.pi / height)
    return (jnp.cos(angles), jnp.sin(angles))


def spectral_backward(spec_grad, weights, modes_y):
    hp = lax.Precision.HIGHEST
    grad_re, grad_im = (spec_grad[..., :modes_y], spec_grad[..., modes_y:])
    weight_re, weight_im = (weights[..., :modes_y], weights[..., modes_y:])
    real_part = jnp.einsum("kbox,kcox->kbcx", grad_re, weight_re, precision=hp) + jnp.einsum(
        "kbox,kcox->kbcx", grad_im, weight_im, precision=hp
    )
    imag_part = jnp.einsum("kbox,kcox->kbcx", grad_im, weight_re, precision=hp) - jnp.einsum(
        "kbox,kcox->kbcx", grad_re, weight_im, precision=hp
    )
    return jnp.concatenate([real_part, imag_part], axis=-1)


def weight_terms(spectrum, spec_grad, modes_y):
    hp = lax.Precision.HIGHEST
    spec_re, spec_im = (spectrum[..., :modes_y], spectrum[..., modes_y:])
    grad_re, grad_im = (spec_grad[..., :modes_y], spec_grad[..., modes_y:])
    real_part = jnp.einsum("kbcx,kbox->kcox", spec_re, grad_re, precision=hp) + jnp.einsum(
        "kbcx,kbox->kcox", spec_im, grad_im, precision=hp
    )
    imag_part = jnp.einsum("kbcx,kbox->kcox", spec_re, grad_im, precision=hp) - jnp.einsum(
        "kbcx,kbox->kcox", spec_im, grad_re, precision=hp
    )
    joined = jnp.concatenate([real_part, imag_part], axis=-1)
    return joined.reshape(joined.shape[0], joined.shape[1] * joined.shape[2], joined.shape[3])


def general_body(cotangent, spectrum, weights):
    hp = lax.Precision.HIGHEST
    space_count = lax.axis_size("space")
    raster_count, channels, row_count, col_count = cotangent.shape
    local_modes = spectrum.shape[0]
    modes_y = spectrum.shape[3] // 2
    height = row_count * space_count
    basis = column_basis(col_count, modes_y)
    first_row = lax.axis_index("space") * row_count
    col_spec = jnp.einsum(
        "rcxw,wj->rcxj", cotangent, basis, precision=hp, preferred_element_type=jnp.float32
    )
    forward_scale = 1.0 / math.sqrt(height * col_count)
    cosines, sines = row_basis(local_modes * lax.axis_size("space"), first_row, row_count, height)
    with_cos = jnp.einsum("kx,rcxj->krcj", cosines, col_spec, precision=hp)
    with_sin = jnp.einsum("kx,rcxj->krcj", sines, col_spec, precision=hp)
    joined = jnp.concatenate(
        [
            with_cos[..., :modes_y] + with_sin[..., modes_y:],
            with_cos[..., modes_y:] - with_sin[..., :modes_y],
        ],
        axis=-1,
    )
    spec_grad = lax.psum_scatter(joined * forward_scale, "space", scatter_dimension=0, tiled=True)
    input_spec = spectral_backward(spec_grad, weights, modes_y)
    local_terms = weight_terms(spectrum, spec_grad, modes_y)
    grad_weights = lax.psum_scatter(local_terms, "dp", scatter_dimension=1, tiled=True)
    shard_piece = lax.all_gather(input_spec, "space", axis=0, tiled=True)
    cosines, sines = row_basis(shard_piece.shape[0], first_row, row_count, height)
    back_cos = jnp.einsum("kx,krcj->rcxj", cosines, shard_piece, precision=hp)
    back_sin = jnp.einsum("kx,krcj->rcxj", sines, shard_piece, precision=hp)
    joined = jnp.concatenate(
        [
            back_cos[..., :modes_y] - back_sin[..., modes_y:],
            back_cos[..., modes_y:] + back_sin[..., :modes_y],
        ],
        axis=-1,
    )
    inverse_scale = 1.0 / math.sqrt(local_modes * space_count * modes_y)
    grad_input = (jnp.einsum("rcxj,wj->rcxw", joined, basis, precision=hp) * inverse_scale).astype(
        jnp.bfloat16
    )
    return (grad_input, grad_weights)


def halves(table):
    high = table.astype(ml_dtypes.bfloat16)
    low = (table - high.astype(np.float64)).astype(ml_dtypes.bfloat16)
    return high, low


def tables(modes, modes_y, rows, cols, space):
    height = rows * space
    angle = 2.0 * np.pi * (np.outer(np.arange(cols), np.arange(modes_y)) % cols) / cols
    high, low = halves(np.concatenate([np.cos(angle), -np.sin(angle)], axis=1))
    into = np.concatenate([high, low], axis=1)
    out_of = np.concatenate([high.T, high.T, low.T], axis=0)
    angle = 2.0 * np.pi * (np.outer(np.arange(modes), np.arange(height)) % height) / height
    cosines = np.cos(angle).reshape(modes, space, rows).transpose(1, 0, 2)
    sines = np.sin(angle).reshape(modes, space, rows).transpose(1, 0, 2)
    high, low = halves(np.concatenate([cosines, sines], axis=2) / math.sqrt(height * cols))
    rows_in = np.concatenate([high, low, high], axis=2)
    order = np.arange(modes).reshape(space, PARTS, -1).transpose(1, 0, 2).reshape(PARTS, -1)
    both = np.concatenate([cosines[:, order], sines[:, order]], axis=2).transpose(0, 1, 3, 2)
    high, low = halves(both / math.sqrt(modes * modes_y))
    rows_out = np.concatenate([high, low, high], axis=3)
    return into, rows_in, rows_out, out_of


def split(values):
    high = values.astype(jnp.bfloat16)
    low = (values - high.astype(jnp.float32)).astype(jnp.bfloat16)
    return high, low


def kernel(
    dp, space,
    cot_hbm, spec_hbm, w_hbm, into_hbm, rows_in_hbm, rows_out_hbm,
    back_hbm, gw_hbm,
    back_ref, gw_ref, cot, spec, w, into, rows_in, rows_out,
    part, rs_in, gall, iall, back_sum, sp_out, sp_in, a_rows, b_rows,
    load_sem, store_sem, rs_send, rs_recv, ag_send, ag_recv, sp_send, sp_recv,
    up_send, down_send, sib_send, g_recv,
):
    me_d = lax.axis_index("dp")
    me_s = lax.axis_index("space")
    channels, rows, cols = cot.shape
    local = w.shape[0]
    modes = local * space
    lanes = w.shape[3]
    half = lanes // 2
    own = channels // dp
    groups = channels // GROUP

    def at(d, s):
        return {"dp": d, "space": s}

    def partner_d(t):
        return lax.rem(me_d + t, dp)

    def partner_s(t):
        return lax.rem(me_s + t, space)

    def source_s(t):
        return lax.rem(me_s + space - t, space)

    barrier = pltpu.get_barrier_semaphore()
    for t in range(1, dp):
        pl.semaphore_signal(barrier, inc=1, device_id=at(partner_d(t), me_s), device_id_type=MESH)
    for t in range(1, space):
        pl.semaphore_signal(barrier, inc=1, device_id=at(me_d, partner_s(t)), device_id_type=MESH)

    def load(n, src, dst):
        copy = pltpu.make_async_copy(src, dst, load_sem.at[n])
        copy.start()
        return copy

    n = 1 + groups
    l_spec = load(n + 1, spec_hbm.at[:, 0], spec)
    l_into = load(0, into_hbm, into)
    l_cot = []
    for g in range(groups):
        place = pl.ds(g * GROUP, GROUP)
        l_cot.append(load(1 + g, cot_hbm.at[0, place], cot.at[place]))
    l_rows_in = load(n, rows_in_hbm.at[me_s], rows_in)
    l_w = load(n + 2, w_hbm, w)
    l_rows_out = load(n + 3, rows_out_hbm.at[me_s], rows_out)

    lane = lax.broadcasted_iota(jnp.int32, (1, lanes), 1)
    lower = lane < half
    sign = jnp.where(lower, 1.0, -1.0).astype(jnp.float32)

    def turn(values):
        return pltpu.roll(values, half, values.ndim - 1)

    size = local // PARTS

    def rs_copy(t, piece):
        there = partner_s(t)
        if piece < groups:
            first, place = 0, pl.ds(piece * GROUP, GROUP)
        else:
            first, place = (piece - groups + 1) * size, pl.ds(0, channels)
        return pltpu.make_async_remote_copy(
            part.at[pl.ds(there * local + first, size), place],
            rs_in.at[t - 1, pl.ds(first, size), place],
            rs_send.at[t - 1, piece],
            rs_recv.at[t - 1, piece],
            device_id=at(me_d, there),
            device_id_type=MESH,
        )

    def sp_copy(t):
        there = partner_d(t)
        return pltpu.make_async_remote_copy(
            sp_out.at[there],
            sp_in.at[me_d],
            sp_send.at[t],
            sp_recv.at[t],
            device_id=at(there, me_s),
            device_id_type=MESH,
        )

    def sp_arrival(t):
        source = lax.rem(me_d + dp - t, dp)
        return pltpu.make_async_remote_copy(
            sp_out.at[source],
            sp_in.at[source],
            sp_send.at[t],
            sp_recv.at[t],
            device_id=at(source, me_s),
            device_id_type=MESH,
        )

    l_spec.wait()
    for d in range(dp):
        for k in range(local):
            sp_out[d, k * own : (k + 1) * own, :] = spec[k, d * own : (d + 1) * own, :]
    pl.semaphore_wait(barrier, dp + space - 2)
    for t in range(1, dp):
        sp_copy(t).start()
    sp_in[me_d] = sp_out[me_d]
    l_into.wait()
    l_rows_in.wait()
    for g in range(groups):
        l_cot[g].wait()
        block = cot[pl.ds(g * GROUP, GROUP)].reshape(GROUP * rows, cols)
        both = jnp.dot(block, into[...], preferred_element_type=jnp.float32)
        col = both[:, :lanes] + both[:, lanes:]
        turned = turn(col) * sign
        stacked = jnp.concatenate(
            [
                jnp.concatenate(
                    [col[i * rows : (i + 1) * rows], turned[i * rows : (i + 1) * rows]], axis=0
                )
                for i in range(GROUP)
            ],
            axis=1,
        )
        high, low = split(stacked)
        spectrum_part = jnp.dot(
            rows_in[...],
            jnp.concatenate([high, high, low], axis=0),
            preferred_element_type=jnp.float32,
        )
        for i in range(GROUP):
            part[:, g * GROUP + i, :] = spectrum_part[:, i * lanes : (i + 1) * lanes]
        for t in range(1, space):
            rs_copy(t, g).start()
    for piece in range(groups, groups + PARTS - 1):
        for t in range(1, space):
            rs_copy(t, piece).start()

    gw_ref[...] = jnp.zeros_like(gw_ref)

    z, core = me_d // 2, lax.rem(me_d, 2)
    nz = dp // 2
    twin = 1 - 2 * core

    def g_copy(b, h, there, sem):
        place = pl.ds(h * size, size)
        return pltpu.make_async_remote_copy(
            gall.at[b, place],
            gall.at[b, place],
            sem.at[b, h],
            g_recv.at[b, h],
            device_id=at(there, me_s),
            device_id_type=MESH,
        )

    def up(b, h):
        return g_copy(b, h, me_d + 2, up_send)

    def down(b, h):
        return g_copy(b, h, me_d - 2, down_send)

    def sibling(b, h):
        return g_copy(b, h, me_d + twin, sib_send)

    def own_sends(h, act):
        @pl.when(z < nz - 1)
        def _():
            act(up(me_d, h))

        @pl.when(z > 0)
        def _():
            act(down(me_d, h))

        act(sibling(me_d, h))

    def passed_on(t, h, act, arrive):
        @pl.when(z >= t)
        def _():
            below = me_d - 2 * t
            if arrive:
                down(below, h).wait_recv()

            @pl.when(z < nz - 1)
            def _():
                act(up(below, h))

            act(sibling(below, h))

        @pl.when(z + t < nz)
        def _():
            above = me_d + 2 * t
            if arrive:
                up(above, h).wait_recv()

            @pl.when(z > 0)
            def _():
                act(down(above, h))

            act(sibling(above, h))

    def forward(t, h):
        passed_on(t, h, lambda copy: copy.start(), True)

    def ag_copy(t, h):
        place = pl.ds(me_s * size, size)
        return pltpu.make_async_remote_copy(
            iall.at[h, place],
            iall.at[h, place],
            ag_send.at[t - 1, h],
            ag_recv.at[t - 1, h],
            device_id=at(me_d, partner_s(t)),
            device_id_type=MESH,
        )

    def ag_arrival(t, h):
        place = pl.ds(source_s(t) * size, size)
        return pltpu.make_async_remote_copy(
            iall.at[h, place],
            iall.at[h, place],
            ag_send.at[t - 1, h],
            ag_recv.at[t - 1, h],
            device_id=at(me_d, source_s(t)),
            device_id_type=MESH,
        )

    def summed(h):
        def gather_sum(k, carry):
            total = part[me_s * local + k]
            for t in range(1, space):
                total = total + rs_in[t - 1, k]
            gall[me_d, k] = total
            return carry

        lax.fori_loop(h * size, (h + 1) * size, gather_sum, 0, unroll=True)
        own_sends(h, lambda copy: copy.start())

    def mixed_by(h):
        def mix(k, carry):
            grad = gall[me_d, k]
            weight = w[k]
            plain = jnp.sum(weight * grad[None], axis=1)
            cross = jnp.sum(weight * turn(grad)[None], axis=1)
            mixed = jnp.where(lower, plain + turn(plain), turn(cross) - cross)
            iall[h, me_s * size + k - h * size] = mixed
            return carry

        lax.fori_loop(h * size, (h + 1) * size, mix, 0, unroll=True)

    def ag_start(h):
        for t in range(1, space):
            ag_copy(t, h).start()

    def rows_of(b):
        saved = sp_in[b]
        a_rows[b] = jnp.where(lower, saved, turn(saved))
        b_rows[b] = jnp.where(lower, turn(saved), -saved)

    def add_terms(blocks, h):
        def one(k, carry):
            grads = [gall[b, k] for b in blocks]
            turned = [turn(grad) for grad in grads]
            for c in range(own):
                row = pl.ds(k * own + c, 1)
                place = pl.ds(c * channels, channels)
                total = gw_ref[k, place, :]
                for b, grad, other in zip(blocks, grads, turned):
                    total = total + (a_rows[b, row, :] * grad + b_rows[b, row, :] * other)
                gw_ref[k, place, :] = total
            return carry

        lax.fori_loop(h * size, (h + 1) * size, one, 0, unroll=True)

    def pair_terms(b, h):
        sibling(b + twin, h).wait_recv()
        add_terms((b, b + twin), h)

    def terms(t, h):
        @pl.when(z >= t)
        def _():
            pair_terms(me_d - 2 * t, h)

        @pl.when(z + t < nz)
        def _():
            pair_terms(me_d + 2 * t, h)

    def rows_back(h):
        for t in range(1, space):
            ag_arrival(t, h).wait_recv()
        for g in range(groups):
            mixed = jnp.concatenate([iall[h, :, g * GROUP + i, :] for i in range(GROUP)], axis=1)
            turned = jnp.concatenate(
                [-sign * turn(mixed[:, i * lanes : (i + 1) * lanes]) for i in range(GROUP)],
                axis=1,
            )
            high, low = split(jnp.concatenate([mixed, turned], axis=0))
            found = jnp.dot(
                rows_out[h],
                jnp.concatenate([high, high, low], axis=0),
                preferred_element_type=jnp.float32,
            )
            place = pl.ds(g * GROUP * lanes, GROUP * lanes)
            if h == 0:
                back_sum[:, place] = found
            elif h < PARTS - 1:
                back_sum[:, place] += found
            else:
                found = back_sum[:, place] + found
                high, low = split(
                    jnp.concatenate(
                        [found[:, i * lanes : (i + 1) * lanes] for i in range(GROUP)], axis=0
                    )
                )
                place = pl.ds(g * GROUP * rows, GROUP * rows)
                back_ref[place, pl.ds(0, lanes)] = high
                back_ref[place, pl.ds(lanes, lanes)] = low
                back_store(g).start()

    def back_store(g):
        place = pl.ds(g * GROUP * rows, GROUP * rows)
        return pltpu.make_async_copy(back_ref.at[place], back_hbm.at[place], store_sem.at[g])

    def gw_store():
        return pltpu.make_async_copy(gw_ref, gw_hbm, store_sem.at[groups])

    def arrived(h):
        for t in range(1, space):
            for piece in range(groups) if h == 0 else (groups + h - 1,):
                rs_copy(t, piece).wait_recv()

    def forward_some(*steps):
        for t, h in steps:
            if t < nz:
                forward(t, h)

    def terms_some(*steps):
        for t, h in steps:
            if t < nz:
                terms(t, h)

    arrived(0)
    summed(0)
    l_w.wait()
    mixed_by(0)
    arrived(1)
    summed(1)
    forward_some((1, 0))
    mixed_by(1)
    arrived(2)
    summed(2)
    forward_some((1, 1), (2, 0))
    mixed_by(2)
    for t in range(1, dp):
        sp_arrival(t).wait_recv()
    for b in range(dp):
        rows_of(b)
    arrived(3)
    for h in range(3):
        ag_start(h)
    summed(3)
    mixed_by(3)
    ag_start(3)
    forward_some((1, 2), (2, 1), (3, 0))
    for h in range(PARTS):
        pair_terms(me_d, h)
    forward_some((1, 3), (2, 2), (3, 1))
    terms_some((1, 0), (1, 1))
    forward_some((2, 3), (3, 2))
    l_rows_out.wait()
    rows_back(0)
    terms_some((1, 2), (1, 3), (2, 0))
    rows_back(1)
    terms_some((2, 1), (3, 0), (2, 2))
    forward_some((3, 3))
    rows_back(2)
    terms_some((3, 1), (2, 3), (3, 2))
    rows_back(3)
    terms_some((3, 3))
    for t in range(4, nz):
        for h in range(PARTS):
            forward(t, h)
            terms(t, h)
    gw_store().start()

    def leave(copy):
        copy.wait_send()

    for t in range(1, space):
        for piece in range(groups + PARTS - 1):
            rs_copy(t, piece).wait_send()
        for h in range(PARTS):
            ag_copy(t, h).wait_send()
    for t in range(1, dp):
        sp_copy(t).wait_send()
    for h in range(PARTS):
        own_sends(h, leave)
        for t in range(1, nz):
            passed_on(t, h, leave, False)
    for g in range(groups):
        back_store(g).wait()
    gw_store().wait()


def columns_kernel(
    back_hbm, terms_hbm, out_of_hbm, gin_hbm, gw_hbm,
    back, terms, out_of, gin, load_sem, store_sem,
):
    channels, rows, cols = gin.shape
    groups = channels // COLUMNS
    lanes = back.shape[1] // 2
    count = COLUMNS * rows
    l_out_of = pltpu.make_async_copy(out_of_hbm, out_of, load_sem.at[groups])
    l_out_of.start()
    loads, stores = [], []
    for g in range(groups):
        place = pl.ds(g * count, count)
        loads.append(pltpu.make_async_copy(back_hbm.at[place], back.at[place], load_sem.at[g]))
        loads[g].start()
    l_terms = pltpu.make_async_copy(terms_hbm, terms, load_sem.at[groups + 1])
    l_terms.start()
    l_out_of.wait()
    for g in range(groups):
        loads[g].wait()
        both = back[pl.ds(g * count, count)]
        raster = jnp.dot(
            jnp.concatenate([both, both[:, :lanes]], axis=1),
            out_of[...],
            preferred_element_type=jnp.float32,
        )
        place = pl.ds(g * COLUMNS, COLUMNS)
        gin[place] = raster.reshape(COLUMNS, rows, cols).astype(jnp.bfloat16)
        stores.append(pltpu.make_async_copy(gin.at[place], gin_hbm.at[0, place], store_sem.at[g]))
        stores[g].start()
        if g == 0:
            l_terms.wait()
            s_terms = pltpu.make_async_copy(terms, gw_hbm, store_sem.at[groups])
            s_terms.start()
    for store in stores:
        store.wait()
    s_terms.wait()


def fused_body(dp, space, cotangent, spectrum, weights):
    _, channels, rows, cols = cotangent.shape
    local, _, _, lanes = spectrum.shape
    modes = local * space
    own = channels // dp
    groups = channels // GROUP
    fixed = [jnp.asarray(t) for t in tables(modes, lanes // 2, rows, cols, space)]
    into, rows_in, rows_out, out_of = fixed
    f32 = jnp.float32
    dma = pltpu.SemaphoreType.DMA
    back, terms = pl.pallas_call(
        functools.partial(kernel, dp, space),
        out_shape=(
            jax.ShapeDtypeStruct((channels * rows, 2 * lanes), jnp.bfloat16),
            jax.ShapeDtypeStruct((local, own * channels, lanes), f32),
        ),
        in_specs=[pl.BlockSpec(memory_space=pl.ANY)] * 6,
        out_specs=[pl.BlockSpec(memory_space=pl.ANY)] * 2,
        scratch_shapes=[
            pltpu.VMEM((channels * rows, 2 * lanes), jnp.bfloat16),
            pltpu.VMEM((local, own * channels, lanes), f32),
            pltpu.VMEM((channels, rows, cols), jnp.bfloat16),
            pltpu.VMEM((local, channels, lanes), f32),
            pltpu.VMEM(weights.shape, f32),
            pltpu.VMEM(into.shape, jnp.bfloat16),
            pltpu.VMEM(rows_in.shape[1:], jnp.bfloat16),
            pltpu.VMEM(rows_out.shape[1:], jnp.bfloat16),
            pltpu.VMEM((modes, channels, lanes), f32),
            pltpu.VMEM((space - 1, local, channels, lanes), f32),
            pltpu.VMEM((dp, local, channels, lanes), f32),
            pltpu.VMEM((PARTS, modes // PARTS, channels, lanes), f32),
            pltpu.VMEM((rows, channels * lanes), f32),
            pltpu.VMEM((dp, local * own, lanes), f32),
            pltpu.VMEM((dp, local * own, lanes), f32),
            pltpu.VMEM((dp, local * own, lanes), f32),
            pltpu.VMEM((dp, local * own, lanes), f32),
            dma((groups + 5,)),
            dma((groups + 2,)),
            dma((space - 1, groups + PARTS - 1)),
            dma((space - 1, groups + PARTS - 1)),
            dma((space - 1, PARTS)),
            dma((space - 1, PARTS)),
            dma((dp,)),
            dma((dp,)),
            dma((dp, PARTS)),
            dma((dp, PARTS)),
            dma((dp, PARTS)),
            dma((dp, PARTS)),
        ],
        compiler_params=pltpu.CompilerParams(
            collective_id=0, has_side_effects=True, vmem_limit_bytes=62 * 1024 * 1024
        ),
    )(cotangent, spectrum, weights, into, rows_in, rows_out)
    return pl.pallas_call(
        columns_kernel,
        out_shape=(
            jax.ShapeDtypeStruct(cotangent.shape, jnp.bfloat16),
            jax.ShapeDtypeStruct(terms.shape, f32),
        ),
        in_specs=[pl.BlockSpec(memory_space=pl.ANY)] * 3,
        out_specs=[pl.BlockSpec(memory_space=pl.ANY)] * 2,
        scratch_shapes=[
            pltpu.VMEM(back.shape, jnp.bfloat16),
            pltpu.VMEM(terms.shape, f32),
            pltpu.VMEM(out_of.shape, jnp.bfloat16),
            pltpu.VMEM(cotangent.shape[1:], jnp.bfloat16),
            dma((channels // COLUMNS + 2,)),
            dma((channels // COLUMNS + 1,)),
        ],
        compiler_params=pltpu.CompilerParams(vmem_limit_bytes=62 * 1024 * 1024),
    )(back, terms, out_of)


def solution(mesh):
    placed = (
        P("dp", None, "space", None),
        P("space", "dp", None, None),
        P("space", None, None, None),
    )
    dp, space = mesh.shape["dp"], mesh.shape["space"]

    def body(cotangent, spectrum, weights):
        rasters, channels, rows, _ = cotangent.shape
        whole_rows = (
            rasters == 1
            and dp % 2 == 0
            and channels % dp == 0
            and channels % GROUP == 0
            and spectrum.shape[0] % PARTS == 0
            and rows % 16 == 0
            and (spectrum.shape[0] * (channels // dp)) % 8 == 0
        )
        if whole_rows:
            return fused_body(dp, space, cotangent, spectrum, weights)
        return general_body(cotangent, spectrum, weights)

    return jax.shard_map(
        body,
        mesh=mesh,
        in_specs=placed,
        out_specs=(P("dp", None, "space", None), P("space", "dp", None)),
        check_vma=False,
    )
```

```python
import functools
import math

import jax
import jax.numpy as jnp
import ml_dtypes
import numpy as np
from jax import lax
from jax.experimental import pallas as pl
from jax.experimental.pallas import tpu as pltpu
from jax.sharding import PartitionSpec as P

MESH = pl.DeviceIdType.MESH
GROUP = 8
COLUMNS = 256


def column_basis(col_count, modes_y):
    position = jnp.arange(col_count, dtype=jnp.int32)
    frequency = jnp.arange(modes_y, dtype=jnp.int32)
    phase = position[:, None] * frequency[None, :] % col_count
    angles = phase.astype(jnp.float32) * (2.0 * math.pi / col_count)
    return jnp.concatenate([jnp.cos(angles), -jnp.sin(angles)], axis=1)


def row_basis(mode_count, first_row, row_count, height):
    frequency = jnp.arange(mode_count, dtype=jnp.int32)
    position = first_row + jnp.arange(row_count, dtype=jnp.int32)
    phase = frequency[:, None] * position[None, :] % height
    angles = phase.astype(jnp.float32) * (2.0 * math.pi / height)
    return (jnp.cos(angles), jnp.sin(angles))


def spectral_backward(spec_grad, weights, modes_y):
    hp = lax.Precision.HIGHEST
    grad_re, grad_im = (spec_grad[..., :modes_y], spec_grad[..., modes_y:])
    weight_re, weight_im = (weights[..., :modes_y], weights[..., modes_y:])
    real_part = jnp.einsum("kbox,kcox->kbcx", grad_re, weight_re, precision=hp) + jnp.einsum(
        "kbox,kcox->kbcx", grad_im, weight_im, precision=hp
    )
    imag_part = jnp.einsum("kbox,kcox->kbcx", grad_im, weight_re, precision=hp) - jnp.einsum(
        "kbox,kcox->kbcx", grad_re, weight_im, precision=hp
    )
    return jnp.concatenate([real_part, imag_part], axis=-1)


def weight_terms(spectrum, spec_grad, modes_y):
    hp = lax.Precision.HIGHEST
    spec_re, spec_im = (spectrum[..., :modes_y], spectrum[..., modes_y:])
    grad_re, grad_im = (spec_grad[..., :modes_y], spec_grad[..., modes_y:])
    real_part = jnp.einsum("kbcx,kbox->kcox", spec_re, grad_re, precision=hp) + jnp.einsum(
        "kbcx,kbox->kcox", spec_im, grad_im, precision=hp
    )
    imag_part = jnp.einsum("kbcx,kbox->kcox", spec_re, grad_im, precision=hp) - jnp.einsum(
        "kbcx,kbox->kcox", spec_im, grad_re, precision=hp
    )
    joined = jnp.concatenate([real_part, imag_part], axis=-1)
    return joined.reshape(joined.shape[0], joined.shape[1] * joined.shape[2], joined.shape[3])


def general_body(cotangent, spectrum, weights):
    hp = lax.Precision.HIGHEST
    space_count = lax.axis_size("space")
    raster_count, channels, row_count, col_count = cotangent.shape
    local_modes = spectrum.shape[0]
    modes_y = spectrum.shape[3] // 2
    height = row_count * space_count
    basis = column_basis(col_count, modes_y)
    first_row = lax.axis_index("space") * row_count
    col_spec = jnp.einsum(
        "rcxw,wj->rcxj", cotangent, basis, precision=hp, preferred_element_type=jnp.float32
    )
    forward_scale = 1.0 / math.sqrt(height * col_count)
    cosines, sines = row_basis(local_modes * lax.axis_size("space"), first_row, row_count, height)
    with_cos = jnp.einsum("kx,rcxj->krcj", cosines, col_spec, precision=hp)
    with_sin = jnp.einsum("kx,rcxj->krcj", sines, col_spec, precision=hp)
    joined = jnp.concatenate(
        [
            with_cos[..., :modes_y] + with_sin[..., modes_y:],
            with_cos[..., modes_y:] - with_sin[..., :modes_y],
        ],
        axis=-1,
    )
    spec_grad = lax.psum_scatter(joined * forward_scale, "space", scatter_dimension=0, tiled=True)
    input_spec = spectral_backward(spec_grad, weights, modes_y)
    local_terms = weight_terms(spectrum, spec_grad, modes_y)
    grad_weights = lax.psum_scatter(local_terms, "dp", scatter_dimension=1, tiled=True)
    shard_piece = lax.all_gather(input_spec, "space", axis=0, tiled=True)
    cosines, sines = row_basis(shard_piece.shape[0], first_row, row_count, height)
    back_cos = jnp.einsum("kx,krcj->rcxj", cosines, shard_piece, precision=hp)
    back_sin = jnp.einsum("kx,krcj->rcxj", sines, shard_piece, precision=hp)
    joined = jnp.concatenate(
        [
            back_cos[..., :modes_y] - back_sin[..., modes_y:],
            back_cos[..., modes_y:] + back_sin[..., :modes_y],
        ],
        axis=-1,
    )
    inverse_scale = 1.0 / math.sqrt(local_modes * space_count * modes_y)
    grad_input = (jnp.einsum("rcxj,wj->rcxw", joined, basis, precision=hp) * inverse_scale).astype(
        jnp.bfloat16
    )
    return (grad_input, grad_weights)


def halves(table):
    high = table.astype(ml_dtypes.bfloat16)
    low = (table - high.astype(np.float64)).astype(ml_dtypes.bfloat16)
    return high, low


def stack(high, low):
    above = np.concatenate([high, high], axis=-1)
    below = np.concatenate([low, np.zeros_like(low)], axis=-1)
    return np.concatenate([above, below], axis=-2)


def tables(modes, modes_y, rows, cols, space):
    height = rows * space
    angle = 2.0 * np.pi * (np.outer(np.arange(cols), np.arange(modes_y)) % cols) / cols
    high, low = halves(np.concatenate([np.cos(angle), -np.sin(angle)], axis=1))
    into = np.concatenate([high, low], axis=1)
    out_of = np.concatenate([high.T, high.T, low.T], axis=0)
    angle = 2.0 * np.pi * (np.outer(np.arange(modes), np.arange(height)) % height) / height
    cosines = np.cos(angle).reshape(modes, space, rows).transpose(1, 0, 2)
    sines = np.sin(angle).reshape(modes, space, rows).transpose(1, 0, 2)
    high, low = halves(np.concatenate([cosines, sines], axis=2) / math.sqrt(height * cols))
    rows_in = stack(high, low)
    local = modes // space
    order = np.arange(modes).reshape(space, 2, local // 2).transpose(1, 0, 2).reshape(2, -1)
    both = np.concatenate([cosines[:, order], sines[:, order]], axis=2).transpose(0, 1, 3, 2)
    high, low = halves(both / math.sqrt(modes * modes_y))
    rows_out = stack(high, low)
    return into, rows_in, rows_out, out_of


def split(values):
    high = values.astype(jnp.bfloat16)
    low = (values - high.astype(jnp.float32)).astype(jnp.bfloat16)
    return high, low


def kernel(
    dp, space,
    cot_hbm, spec_hbm, w_hbm, into_hbm, rows_in_hbm, rows_out_hbm,
    back_hbm, gw_hbm,
    back_ref, gw_ref, cot, spec, w, into, rows_in, rows_out,
    part, rs_in, gall, iall, back_sum, sp_out, sp_in, a_rows, b_rows,
    load_sem, store_sem, rs_send, rs_recv, ag_send, ag_recv, sp_send, sp_recv,
    up_send, down_send, sib_send, g_recv,
):
    me_d = lax.axis_index("dp")
    me_s = lax.axis_index("space")
    channels, rows, cols = cot.shape
    local = w.shape[0]
    modes = local * space
    lanes = w.shape[3]
    half = lanes // 2
    own = channels // dp
    groups = channels // GROUP

    def at(d, s):
        return {"dp": d, "space": s}

    def partner_d(t):
        return lax.rem(me_d + t, dp)

    def partner_s(t):
        return lax.rem(me_s + t, space)

    def source_s(t):
        return lax.rem(me_s + space - t, space)

    barrier = pltpu.get_barrier_semaphore()
    for t in range(1, dp):
        pl.semaphore_signal(barrier, inc=1, device_id=at(partner_d(t), me_s), device_id_type=MESH)
    for t in range(1, space):
        pl.semaphore_signal(barrier, inc=1, device_id=at(me_d, partner_s(t)), device_id_type=MESH)

    def load(n, src, dst):
        copy = pltpu.make_async_copy(src, dst, load_sem.at[n])
        copy.start()
        return copy

    l_into = load(0, into_hbm, into)
    l_cot = []
    for g in range(groups):
        place = pl.ds(g * GROUP, GROUP)
        l_cot.append(load(1 + g, cot_hbm.at[0, place], cot.at[place]))
    n = 1 + groups
    l_rows_in = load(n, rows_in_hbm.at[me_s], rows_in)
    l_spec = load(n + 1, spec_hbm.at[:, 0], spec)
    l_w = load(n + 2, w_hbm, w)
    l_rows_out = load(n + 3, rows_out_hbm.at[me_s], rows_out)

    lane = lax.broadcasted_iota(jnp.int32, (1, lanes), 1)
    lower = lane < half
    sign = jnp.where(lower, 1.0, -1.0).astype(jnp.float32)

    def turn(values):
        return pltpu.roll(values, half, values.ndim - 1)

    size = local // 2

    def rs_copy(t, piece):
        there = partner_s(t)
        if piece < groups:
            first, place = 0, pl.ds(piece * GROUP, GROUP)
        else:
            first, place = size, pl.ds(0, channels)
        return pltpu.make_async_remote_copy(
            part.at[pl.ds(there * local + first, size), place],
            rs_in.at[t - 1, pl.ds(first, size), place],
            rs_send.at[t - 1, piece],
            rs_recv.at[t - 1, piece],
            device_id=at(me_d, there),
            device_id_type=MESH,
        )

    def sp_copy(t):
        there = partner_d(t)
        return pltpu.make_async_remote_copy(
            sp_out.at[there],
            sp_in.at[me_d],
            sp_send.at[t],
            sp_recv.at[t],
            device_id=at(there, me_s),
            device_id_type=MESH,
        )

    def sp_arrival(t):
        source = lax.rem(me_d + dp - t, dp)
        return pltpu.make_async_remote_copy(
            sp_out.at[source],
            sp_in.at[source],
            sp_send.at[t],
            sp_recv.at[t],
            device_id=at(source, me_s),
            device_id_type=MESH,
        )

    def send_spectrum():
        l_spec.wait()
        for d in range(dp):
            for k in range(local):
                sp_out[d, k * own : (k + 1) * own, :] = spec[k, d * own : (d + 1) * own, :]
        for t in range(1, dp):
            sp_copy(t).start()
        sp_in[me_d] = sp_out[me_d]

    l_into.wait()
    l_rows_in.wait()
    for g in range(groups):
        l_cot[g].wait()
        block = cot[pl.ds(g * GROUP, GROUP)].reshape(GROUP * rows, cols)
        both = jnp.dot(block, into[...], preferred_element_type=jnp.float32)
        col = both[:, :lanes] + both[:, lanes:]
        turned = turn(col) * sign
        stacked = jnp.concatenate(
            [
                jnp.concatenate(
                    [col[i * rows : (i + 1) * rows], turned[i * rows : (i + 1) * rows]], axis=0
                )
                for i in range(GROUP)
            ],
            axis=1,
        )
        high, low = split(stacked)
        spectrum_part = jnp.dot(
            rows_in[...],
            jnp.concatenate([high, low], axis=0),
            preferred_element_type=jnp.float32,
        )
        spectrum_part = spectrum_part[:modes] + spectrum_part[modes:]
        for i in range(GROUP):
            part[:, g * GROUP + i, :] = spectrum_part[:, i * lanes : (i + 1) * lanes]
        if g == 0:
            pl.semaphore_wait(barrier, dp + space - 2)
        for t in range(1, space):
            rs_copy(t, g).start()
        if g == 0:
            send_spectrum()
    for t in range(1, space):
        rs_copy(t, groups).start()

    gw_ref[...] = jnp.zeros_like(gw_ref)

    z, core = me_d // 2, lax.rem(me_d, 2)
    nz = dp // 2
    twin = 1 - 2 * core

    def g_copy(b, h, there, sem):
        place = pl.ds(h * size, size)
        return pltpu.make_async_remote_copy(
            gall.at[b, place],
            gall.at[b, place],
            sem.at[b, h],
            g_recv.at[b, h],
            device_id=at(there, me_s),
            device_id_type=MESH,
        )

    def up(b, h):
        return g_copy(b, h, me_d + 2, up_send)

    def down(b, h):
        return g_copy(b, h, me_d - 2, down_send)

    def sibling(b, h):
        return g_copy(b, h, me_d + twin, sib_send)

    def own_sends(h, act):
        @pl.when(z < nz - 1)
        def _():
            act(up(me_d, h))

        @pl.when(z > 0)
        def _():
            act(down(me_d, h))

        act(sibling(me_d, h))

    def passed_on(t, h, act, arrive):
        @pl.when(z >= t)
        def _():
            below = me_d - 2 * t
            if arrive:
                down(below, h).wait_recv()

            @pl.when(z < nz - 1)
            def _():
                act(up(below, h))

            act(sibling(below, h))

        @pl.when(z + t < nz)
        def _():
            above = me_d + 2 * t
            if arrive:
                up(above, h).wait_recv()

            @pl.when(z > 0)
            def _():
                act(down(above, h))

            act(sibling(above, h))

    def forward(t, h):
        passed_on(t, h, lambda copy: copy.start(), True)

    def ag_copy(t, h):
        place = pl.ds(me_s * size, size)
        return pltpu.make_async_remote_copy(
            iall.at[h, place],
            iall.at[h, place],
            ag_send.at[t - 1, h],
            ag_recv.at[t - 1, h],
            device_id=at(me_d, partner_s(t)),
            device_id_type=MESH,
        )

    def ag_arrival(t, h):
        place = pl.ds(source_s(t) * size, size)
        return pltpu.make_async_remote_copy(
            iall.at[h, place],
            iall.at[h, place],
            ag_send.at[t - 1, h],
            ag_recv.at[t - 1, h],
            device_id=at(me_d, source_s(t)),
            device_id_type=MESH,
        )

    def summed(h):
        def gather_sum(k, carry):
            total = part[me_s * local + k]
            for t in range(1, space):
                total = total + rs_in[t - 1, k]
            gall[me_d, k] = total
            return carry

        lax.fori_loop(h * size, (h + 1) * size, gather_sum, 0, unroll=True)
        own_sends(h, lambda copy: copy.start())

    def mixed_by(h):
        def mix(k, carry):
            grad = gall[me_d, k]
            weight = w[k]
            plain = jnp.sum(weight * grad[None], axis=1)
            cross = jnp.sum(weight * turn(grad)[None], axis=1)
            mixed = jnp.where(lower, plain + turn(plain), turn(cross) - cross)
            iall[h, me_s * size + k - h * size] = mixed
            return carry

        lax.fori_loop(h * size, (h + 1) * size, mix, 0, unroll=True)

    def ag_start(h):
        for t in range(1, space):
            ag_copy(t, h).start()

    def rows_of(b):
        saved = sp_in[b]
        a_rows[b] = jnp.where(lower, saved, turn(saved))
        b_rows[b] = jnp.where(lower, turn(saved), -saved)

    def add_terms(blocks, h):
        def one(k, carry):
            grads = [gall[b, k] for b in blocks]
            turned = [turn(grad) for grad in grads]
            for c in range(own):
                row = pl.ds(k * own + c, 1)
                place = pl.ds(c * channels, channels)
                total = gw_ref[k, place, :]
                for b, grad, other in zip(blocks, grads, turned):
                    total = total + (a_rows[b, row, :] * grad + b_rows[b, row, :] * other)
                gw_ref[k, place, :] = total
            return carry

        lax.fori_loop(h * size, (h + 1) * size, one, 0, unroll=True)

    def pair_terms(b, h):
        sibling(b + twin, h).wait_recv()
        add_terms((b, b + twin), h)

    def terms(t, h):
        @pl.when(z >= t)
        def _():
            pair_terms(me_d - 2 * t, h)

        @pl.when(z + t < nz)
        def _():
            pair_terms(me_d + 2 * t, h)

    def rows_back(h):
        for t in range(1, space):
            ag_arrival(t, h).wait_recv()
        for g in range(groups):
            mixed = jnp.concatenate([iall[h, :, g * GROUP + i, :] for i in range(GROUP)], axis=1)
            turned = jnp.concatenate(
                [-sign * turn(mixed[:, i * lanes : (i + 1) * lanes]) for i in range(GROUP)],
                axis=1,
            )
            high, low = split(jnp.concatenate([mixed, turned], axis=0))
            found = jnp.dot(
                rows_out[h],
                jnp.concatenate([high, low], axis=0),
                preferred_element_type=jnp.float32,
            )
            found = found[:rows] + found[rows:]
            place = pl.ds(g * GROUP * lanes, GROUP * lanes)
            if h == 0:
                back_sum[:, place] = found
            else:
                found = back_sum[:, place] + found
                high, low = split(
                    jnp.concatenate(
                        [found[:, i * lanes : (i + 1) * lanes] for i in range(GROUP)], axis=0
                    )
                )
                place = pl.ds(g * GROUP * rows, GROUP * rows)
                back_ref[place, pl.ds(0, lanes)] = high
                back_ref[place, pl.ds(lanes, lanes)] = low
                back_store(g).start()

    def back_store(g):
        place = pl.ds(g * GROUP * rows, GROUP * rows)
        return pltpu.make_async_copy(back_ref.at[place], back_hbm.at[place], store_sem.at[g])

    def gw_store(h):
        place = pl.ds(h * size, size)
        return pltpu.make_async_copy(
            gw_ref.at[place], gw_hbm.at[place], store_sem.at[groups + h]
        )

    for t in range(1, space):
        for piece in range(groups):
            rs_copy(t, piece).wait_recv()
    summed(0)
    l_w.wait()
    mixed_by(0)
    forward(1, 0)
    for t in range(1, dp):
        sp_arrival(t).wait_recv()
    for b in range(dp):
        rows_of(b)
    for t in range(1, space):
        rs_copy(t, groups).wait_recv()
    ag_start(0)
    summed(1)
    mixed_by(1)
    ag_start(1)
    if nz > 2:
        forward(2, 0)
    pair_terms(me_d, 0)
    pair_terms(me_d, 1)
    forward(1, 1)
    terms(1, 0)
    if nz > 3:
        forward(3, 0)
    if nz > 2:
        forward(2, 1)
    l_rows_out.wait()
    rows_back(0)
    terms(1, 1)
    if nz > 2:
        terms(2, 0)
    if nz > 3:
        terms(3, 0)
        forward(3, 1)
    rows_back(1)
    if nz > 2:
        terms(2, 1)
    if nz > 3:
        terms(3, 1)
    for t in range(4, nz):
        for h in range(2):
            forward(t, h)
            terms(t, h)
    for h in range(2):
        gw_store(h).start()

    def leave(copy):
        copy.wait_send()

    for t in range(1, space):
        for piece in range(groups + 1):
            rs_copy(t, piece).wait_send()
        for h in range(2):
            ag_copy(t, h).wait_send()
    for t in range(1, dp):
        sp_copy(t).wait_send()
    for h in range(2):
        own_sends(h, leave)
        for t in range(1, nz):
            passed_on(t, h, leave, False)
    for g in range(groups):
        back_store(g).wait()
    for h in range(2):
        gw_store(h).wait()


def columns_kernel(
    back_hbm, terms_hbm, out_of_hbm, gin_hbm, gw_hbm,
    back, terms, out_of, gin, load_sem, store_sem,
):
    channels, rows, cols = gin.shape
    lanes = back.shape[1] // 2
    pieces = cols // COLUMNS
    l_back = pltpu.make_async_copy(back_hbm, back, load_sem.at[pieces])
    l_back.start()
    loads, stores = [], []
    for g in range(pieces):
        place = pl.ds(g * COLUMNS, COLUMNS)
        loads.append(
            pltpu.make_async_copy(out_of_hbm.at[:, place], out_of.at[:, place], load_sem.at[g])
        )
        loads[g].start()
    l_terms = pltpu.make_async_copy(terms_hbm, terms, load_sem.at[pieces + 1])
    l_terms.start()
    l_back.wait()
    both = back[...]
    both = jnp.concatenate([both, both[:, :lanes]], axis=1)
    for g in range(pieces):
        loads[g].wait()
        place = pl.ds(g * COLUMNS, COLUMNS)
        raster = jnp.dot(both, out_of[:, place], preferred_element_type=jnp.float32)
        gin[:, :, place] = raster.reshape(channels, rows, COLUMNS).astype(jnp.bfloat16)
        stores.append(
            pltpu.make_async_copy(gin.at[:, :, place], gin_hbm.at[0, :, :, place], store_sem.at[g])
        )
        stores[g].start()
        if g == 0:
            l_terms.wait()
            s_terms = pltpu.make_async_copy(terms, gw_hbm, store_sem.at[pieces])
            s_terms.start()
    for store in stores:
        store.wait()
    s_terms.wait()


def fused_body(dp, space, cotangent, spectrum, weights):
    _, channels, rows, cols = cotangent.shape
    local, _, _, lanes = spectrum.shape
    modes = local * space
    own = channels // dp
    groups = channels // GROUP
    fixed = [jnp.asarray(t) for t in tables(modes, lanes // 2, rows, cols, space)]
    into, rows_in, rows_out, out_of = fixed
    f32 = jnp.float32
    dma = pltpu.SemaphoreType.DMA
    back, terms = pl.pallas_call(
        functools.partial(kernel, dp, space),
        out_shape=(
            jax.ShapeDtypeStruct((channels * rows, 2 * lanes), jnp.bfloat16),
            jax.ShapeDtypeStruct((local, own * channels, lanes), f32),
        ),
        in_specs=[pl.BlockSpec(memory_space=pl.ANY)] * 6,
        out_specs=[pl.BlockSpec(memory_space=pl.ANY)] * 2,
        scratch_shapes=[
            pltpu.VMEM((channels * rows, 2 * lanes), jnp.bfloat16),
            pltpu.VMEM((local, own * channels, lanes), f32),
            pltpu.VMEM((channels, rows, cols), jnp.bfloat16),
            pltpu.VMEM((local, channels, lanes), f32),
            pltpu.VMEM(weights.shape, f32),
            pltpu.VMEM(into.shape, jnp.bfloat16),
            pltpu.VMEM(rows_in.shape[1:], jnp.bfloat16),
            pltpu.VMEM(rows_out.shape[1:], jnp.bfloat16),
            pltpu.VMEM((modes, channels, lanes), f32),
            pltpu.VMEM((space - 1, local, channels, lanes), f32),
            pltpu.VMEM((dp, local, channels, lanes), f32),
            pltpu.VMEM((2, modes // 2, channels, lanes), f32),
            pltpu.VMEM((rows, channels * lanes), f32),
            pltpu.VMEM((dp, local * own, lanes), f32),
            pltpu.VMEM((dp, local * own, lanes), f32),
            pltpu.VMEM((dp, local * own, lanes), f32),
            pltpu.VMEM((dp, local * own, lanes), f32),
            dma((groups + 5,)),
            dma((groups + 2,)),
            dma((space - 1, groups + 1)),
            dma((space - 1, groups + 1)),
            dma((space - 1, 2)),
            dma((space - 1, 2)),
            dma((dp,)),
            dma((dp,)),
            dma((dp, 2)),
            dma((dp, 2)),
            dma((dp, 2)),
            dma((dp, 2)),
        ],
        compiler_params=pltpu.CompilerParams(
            collective_id=0, has_side_effects=True, vmem_limit_bytes=62 * 1024 * 1024
        ),
    )(cotangent, spectrum, weights, into, rows_in, rows_out)
    return pl.pallas_call(
        columns_kernel,
        out_shape=(
            jax.ShapeDtypeStruct(cotangent.shape, jnp.bfloat16),
            jax.ShapeDtypeStruct(terms.shape, f32),
        ),
        in_specs=[pl.BlockSpec(memory_space=pl.ANY)] * 3,
        out_specs=[pl.BlockSpec(memory_space=pl.ANY)] * 2,
        scratch_shapes=[
            pltpu.VMEM(back.shape, jnp.bfloat16),
            pltpu.VMEM(terms.shape, f32),
            pltpu.VMEM(out_of.shape, jnp.bfloat16),
            pltpu.VMEM(cotangent.shape[1:], jnp.bfloat16),
            dma((cols // COLUMNS + 2,)),
            dma((cols // COLUMNS + 1,)),
        ],
        compiler_params=pltpu.CompilerParams(vmem_limit_bytes=62 * 1024 * 1024),
    )(back, terms, out_of)


def solution(mesh):
    placed = (
        P("dp", None, "space", None),
        P("space", "dp", None, None),
        P("space", None, None, None),
    )
    dp, space = mesh.shape["dp"], mesh.shape["space"]

    def body(cotangent, spectrum, weights):
        rasters, channels, rows, _ = cotangent.shape
        whole_rows = (
            rasters == 1
            and dp % 2 == 0
            and channels % dp == 0
            and channels % GROUP == 0
            and cotangent.shape[3] % COLUMNS == 0
            and spectrum.shape[0] % 2 == 0
            and rows % 16 == 0
            and (spectrum.shape[0] * (channels // dp)) % 8 == 0
        )
        if whole_rows:
            return fused_body(dp, space, cotangent, spectrum, weights)
        return general_body(cotangent, spectrum, weights)

    return jax.shard_map(
        body,
        mesh=mesh,
        in_specs=placed,
        out_specs=(P("dp", None, "space", None), P("space", "dp", None)),
        check_vma=False,
    )
```

```python
import functools
import math

import jax
import jax.numpy as jnp
import ml_dtypes
import numpy as np
from jax import lax
from jax.experimental import pallas as pl
from jax.experimental.pallas import tpu as pltpu
from jax.sharding import PartitionSpec as P

MESH = pl.DeviceIdType.MESH
GROUP = 8


def column_basis(col_count, modes_y):
    position = jnp.arange(col_count, dtype=jnp.int32)
    frequency = jnp.arange(modes_y, dtype=jnp.int32)
    phase = position[:, None] * frequency[None, :] % col_count
    angles = phase.astype(jnp.float32) * (2.0 * math.pi / col_count)
    return jnp.concatenate([jnp.cos(angles), -jnp.sin(angles)], axis=1)


def row_basis(mode_count, first_row, row_count, height):
    frequency = jnp.arange(mode_count, dtype=jnp.int32)
    position = first_row + jnp.arange(row_count, dtype=jnp.int32)
    phase = frequency[:, None] * position[None, :] % height
    angles = phase.astype(jnp.float32) * (2.0 * math.pi / height)
    return (jnp.cos(angles), jnp.sin(angles))


def spectral_backward(spec_grad, weights, modes_y):
    hp = lax.Precision.HIGHEST
    grad_re, grad_im = (spec_grad[..., :modes_y], spec_grad[..., modes_y:])
    weight_re, weight_im = (weights[..., :modes_y], weights[..., modes_y:])
    real_part = jnp.einsum("kbox,kcox->kbcx", grad_re, weight_re, precision=hp) + jnp.einsum(
        "kbox,kcox->kbcx", grad_im, weight_im, precision=hp
    )
    imag_part = jnp.einsum("kbox,kcox->kbcx", grad_im, weight_re, precision=hp) - jnp.einsum(
        "kbox,kcox->kbcx", grad_re, weight_im, precision=hp
    )
    return jnp.concatenate([real_part, imag_part], axis=-1)


def weight_terms(spectrum, spec_grad, modes_y):
    hp = lax.Precision.HIGHEST
    spec_re, spec_im = (spectrum[..., :modes_y], spectrum[..., modes_y:])
    grad_re, grad_im = (spec_grad[..., :modes_y], spec_grad[..., modes_y:])
    real_part = jnp.einsum("kbcx,kbox->kcox", spec_re, grad_re, precision=hp) + jnp.einsum(
        "kbcx,kbox->kcox", spec_im, grad_im, precision=hp
    )
    imag_part = jnp.einsum("kbcx,kbox->kcox", spec_re, grad_im, precision=hp) - jnp.einsum(
        "kbcx,kbox->kcox", spec_im, grad_re, precision=hp
    )
    joined = jnp.concatenate([real_part, imag_part], axis=-1)
    return joined.reshape(joined.shape[0], joined.shape[1] * joined.shape[2], joined.shape[3])


def general_body(cotangent, spectrum, weights):
    hp = lax.Precision.HIGHEST
    space_count = lax.axis_size("space")
    raster_count, channels, row_count, col_count = cotangent.shape
    local_modes = spectrum.shape[0]
    modes_y = spectrum.shape[3] // 2
    height = row_count * space_count
    basis = column_basis(col_count, modes_y)
    first_row = lax.axis_index("space") * row_count
    col_spec = jnp.einsum(
        "rcxw,wj->rcxj", cotangent, basis, precision=hp, preferred_element_type=jnp.float32
    )
    forward_scale = 1.0 / math.sqrt(height * col_count)
    cosines, sines = row_basis(local_modes * lax.axis_size("space"), first_row, row_count, height)
    with_cos = jnp.einsum("kx,rcxj->krcj", cosines, col_spec, precision=hp)
    with_sin = jnp.einsum("kx,rcxj->krcj", sines, col_spec, precision=hp)
    joined = jnp.concatenate(
        [
            with_cos[..., :modes_y] + with_sin[..., modes_y:],
            with_cos[..., modes_y:] - with_sin[..., :modes_y],
        ],
        axis=-1,
    )
    spec_grad = lax.psum_scatter(joined * forward_scale, "space", scatter_dimension=0, tiled=True)
    input_spec = spectral_backward(spec_grad, weights, modes_y)
    local_terms = weight_terms(spectrum, spec_grad, modes_y)
    grad_weights = lax.psum_scatter(local_terms, "dp", scatter_dimension=1, tiled=True)
    shard_piece = lax.all_gather(input_spec, "space", axis=0, tiled=True)
    cosines, sines = row_basis(shard_piece.shape[0], first_row, row_count, height)
    back_cos = jnp.einsum("kx,krcj->rcxj", cosines, shard_piece, precision=hp)
    back_sin = jnp.einsum("kx,krcj->rcxj", sines, shard_piece, precision=hp)
    joined = jnp.concatenate(
        [
            back_cos[..., :modes_y] - back_sin[..., modes_y:],
            back_cos[..., modes_y:] + back_sin[..., :modes_y],
        ],
        axis=-1,
    )
    inverse_scale = 1.0 / math.sqrt(local_modes * space_count * modes_y)
    grad_input = (jnp.einsum("rcxj,wj->rcxw", joined, basis, precision=hp) * inverse_scale).astype(
        jnp.bfloat16
    )
    return (grad_input, grad_weights)


def halves(table):
    high = table.astype(ml_dtypes.bfloat16)
    low = (table - high.astype(np.float64)).astype(ml_dtypes.bfloat16)
    return high, low


def stack(high, low):
    above = np.concatenate([high, high], axis=-1)
    below = np.concatenate([low, np.zeros_like(low)], axis=-1)
    return np.concatenate([above, below], axis=-2)


def tables(modes, modes_y, rows, cols, space):
    height = rows * space
    angle = 2.0 * np.pi * (np.outer(np.arange(cols), np.arange(modes_y)) % cols) / cols
    high, low = halves(np.concatenate([np.cos(angle), -np.sin(angle)], axis=1))
    into = np.concatenate([high, low], axis=1)
    out_of = np.concatenate([high.T, high.T, low.T], axis=0)
    angle = 2.0 * np.pi * (np.outer(np.arange(modes), np.arange(height)) % height) / height
    cosines = np.cos(angle).reshape(modes, space, rows).transpose(1, 0, 2)
    sines = np.sin(angle).reshape(modes, space, rows).transpose(1, 0, 2)
    high, low = halves(np.concatenate([cosines, sines], axis=2) / math.sqrt(height * cols))
    rows_in = stack(high, low)
    local = modes // space
    order = np.arange(modes).reshape(space, 2, local // 2).transpose(1, 0, 2).reshape(2, -1)
    both = np.concatenate([cosines[:, order], sines[:, order]], axis=2).transpose(0, 1, 3, 2)
    high, low = halves(both / math.sqrt(modes * modes_y))
    rows_out = stack(high, low)
    return into, rows_in, rows_out, out_of


def split(values):
    high = values.astype(jnp.bfloat16)
    low = (values - high.astype(jnp.float32)).astype(jnp.bfloat16)
    return high, low


def kernel(
    dp, space,
    cot_hbm, spec_hbm, w_hbm, into_hbm, rows_in_hbm, rows_out_hbm,
    back_hbm, gw_hbm,
    back_ref, gw_ref, cot, spec, w, into, rows_in, rows_out,
    part, rs_in, gall, iall, back_sum, sp_out, sp_in, a_rows, b_rows,
    load_sem, store_sem, rs_send, rs_recv, ag_send, ag_recv, sp_send, sp_recv,
    up_send, down_send, sib_send, g_recv,
):
    me_d = lax.axis_index("dp")
    me_s = lax.axis_index("space")
    channels, rows, cols = cot.shape
    local = w.shape[0]
    modes = local * space
    lanes = w.shape[3]
    half = lanes // 2
    own = channels // dp
    groups = channels // GROUP

    def at(d, s):
        return {"dp": d, "space": s}

    def partner_d(t):
        return lax.rem(me_d + t, dp)

    def partner_s(t):
        return lax.rem(me_s + t, space)

    def source_s(t):
        return lax.rem(me_s + space - t, space)

    barrier = pltpu.get_barrier_semaphore()
    for t in range(1, dp):
        pl.semaphore_signal(barrier, inc=1, device_id=at(partner_d(t), me_s), device_id_type=MESH)
    for t in range(1, space):
        pl.semaphore_signal(barrier, inc=1, device_id=at(me_d, partner_s(t)), device_id_type=MESH)

    def load(n, src, dst):
        copy = pltpu.make_async_copy(src, dst, load_sem.at[n])
        copy.start()
        return copy

    l_into = load(0, into_hbm, into)
    l_cot = []
    for g in range(groups):
        place = pl.ds(g * GROUP, GROUP)
        l_cot.append(load(1 + g, cot_hbm.at[0, place], cot.at[place]))
    n = 1 + groups
    l_rows_in = load(n, rows_in_hbm.at[me_s], rows_in)
    l_spec = load(n + 1, spec_hbm.at[:, 0], spec)
    l_w = load(n + 2, w_hbm, w)
    l_rows_out = load(n + 3, rows_out_hbm.at[me_s], rows_out)

    lane = lax.broadcasted_iota(jnp.int32, (1, lanes), 1)
    lower = lane < half
    sign = jnp.where(lower, 1.0, -1.0).astype(jnp.float32)

    def turn(values):
        return pltpu.roll(values, half, values.ndim - 1)

    size = local // 2

    def rs_copy(t, piece):
        there = partner_s(t)
        if piece < groups:
            first, place = 0, pl.ds(piece * GROUP, GROUP)
        else:
            first, place = size, pl.ds(0, channels)
        return pltpu.make_async_remote_copy(
            part.at[pl.ds(there * local + first, size), place],
            rs_in.at[t - 1, pl.ds(first, size), place],
            rs_send.at[t - 1, piece],
            rs_recv.at[t - 1, piece],
            device_id=at(me_d, there),
            device_id_type=MESH,
        )

    def sp_copy(t):
        there = partner_d(t)
        return pltpu.make_async_remote_copy(
            sp_out.at[there],
            sp_in.at[me_d],
            sp_send.at[t],
            sp_recv.at[t],
            device_id=at(there, me_s),
            device_id_type=MESH,
        )

    def sp_arrival(t):
        source = lax.rem(me_d + dp - t, dp)
        return pltpu.make_async_remote_copy(
            sp_out.at[source],
            sp_in.at[source],
            sp_send.at[t],
            sp_recv.at[t],
            device_id=at(source, me_s),
            device_id_type=MESH,
        )

    def send_spectrum():
        l_spec.wait()
        for d in range(dp):
            for k in range(local):
                sp_out[d, k * own : (k + 1) * own, :] = spec[k, d * own : (d + 1) * own, :]
        for t in range(1, dp):
            sp_copy(t).start()
        sp_in[me_d] = sp_out[me_d]

    l_into.wait()
    l_rows_in.wait()
    for g in range(groups):
        l_cot[g].wait()
        block = cot[pl.ds(g * GROUP, GROUP)].reshape(GROUP * rows, cols)
        both = jnp.dot(block, into[...], preferred_element_type=jnp.float32)
        col = both[:, :lanes] + both[:, lanes:]
        turned = turn(col) * sign
        stacked = jnp.concatenate(
            [
                jnp.concatenate(
                    [col[i * rows : (i + 1) * rows], turned[i * rows : (i + 1) * rows]], axis=0
                )
                for i in range(GROUP)
            ],
            axis=1,
        )
        high, low = split(stacked)
        spectrum_part = jnp.dot(
            rows_in[...],
            jnp.concatenate([high, low], axis=0),
            preferred_element_type=jnp.float32,
        )
        spectrum_part = spectrum_part[:modes] + spectrum_part[modes:]
        for i in range(GROUP):
            part[:, g * GROUP + i, :] = spectrum_part[:, i * lanes : (i + 1) * lanes]
        if g == 0:
            pl.semaphore_wait(barrier, dp + space - 2)
        for t in range(1, space):
            rs_copy(t, g).start()
        if g == 0:
            send_spectrum()
    for t in range(1, space):
        rs_copy(t, groups).start()

    gw_ref[...] = jnp.zeros_like(gw_ref)

    z, core = me_d // 2, lax.rem(me_d, 2)
    nz = dp // 2
    twin = 1 - 2 * core

    def g_copy(b, h, there, sem):
        place = pl.ds(h * size, size)
        return pltpu.make_async_remote_copy(
            gall.at[b, place],
            gall.at[b, place],
            sem.at[b, h],
            g_recv.at[b, h],
            device_id=at(there, me_s),
            device_id_type=MESH,
        )

    def up(b, h):
        return g_copy(b, h, me_d + 2, up_send)

    def down(b, h):
        return g_copy(b, h, me_d - 2, down_send)

    def sibling(b, h):
        return g_copy(b, h, me_d + twin, sib_send)

    def own_sends(h, act):
        @pl.when(z < nz - 1)
        def _():
            act(up(me_d, h))

        @pl.when(z > 0)
        def _():
            act(down(me_d, h))

        act(sibling(me_d, h))

    def passed_on(t, h, act, arrive):
        @pl.when(z >= t)
        def _():
            below = me_d - 2 * t
            if arrive:
                down(below, h).wait_recv()

            @pl.when(z < nz - 1)
            def _():
                act(up(below, h))

            act(sibling(below, h))

        @pl.when(z + t < nz)
        def _():
            above = me_d + 2 * t
            if arrive:
                up(above, h).wait_recv()

            @pl.when(z > 0)
            def _():
                act(down(above, h))

            act(sibling(above, h))

    def forward(t, h):
        passed_on(t, h, lambda copy: copy.start(), True)

    def ag_copy(t, h):
        place = pl.ds(me_s * size, size)
        return pltpu.make_async_remote_copy(
            iall.at[h, place],
            iall.at[h, place],
            ag_send.at[t - 1, h],
            ag_recv.at[t - 1, h],
            device_id=at(me_d, partner_s(t)),
            device_id_type=MESH,
        )

    def ag_arrival(t, h):
        place = pl.ds(source_s(t) * size, size)
        return pltpu.make_async_remote_copy(
            iall.at[h, place],
            iall.at[h, place],
            ag_send.at[t - 1, h],
            ag_recv.at[t - 1, h],
            device_id=at(me_d, source_s(t)),
            device_id_type=MESH,
        )

    def summed(h):
        def gather_sum(k, carry):
            total = part[me_s * local + k]
            for t in range(1, space):
                total = total + rs_in[t - 1, k]
            gall[me_d, k] = total
            return carry

        lax.fori_loop(h * size, (h + 1) * size, gather_sum, 0, unroll=True)
        own_sends(h, lambda copy: copy.start())

    def mixed_by(h):
        def mix(k, carry):
            grad = gall[me_d, k]
            weight = w[k]
            plain = jnp.sum(weight * grad[None], axis=1)
            cross = jnp.sum(weight * turn(grad)[None], axis=1)
            mixed = jnp.where(lower, plain + turn(plain), turn(cross) - cross)
            iall[h, me_s * size + k - h * size] = mixed
            return carry

        lax.fori_loop(h * size, (h + 1) * size, mix, 0, unroll=True)

    def ag_start(h):
        for t in range(1, space):
            ag_copy(t, h).start()

    def rows_of(b):
        saved = sp_in[b]
        a_rows[b] = jnp.where(lower, saved, turn(saved))
        b_rows[b] = jnp.where(lower, turn(saved), -saved)

    def add_terms(blocks, h):
        def one(k, carry):
            grads = [gall[b, k] for b in blocks]
            turned = [turn(grad) for grad in grads]
            for c in range(own):
                row = pl.ds(k * own + c, 1)
                place = pl.ds(c * channels, channels)
                total = gw_ref[k, place, :]
                for b, grad, other in zip(blocks, grads, turned):
                    total = total + (a_rows[b, row, :] * grad + b_rows[b, row, :] * other)
                gw_ref[k, place, :] = total
            return carry

        lax.fori_loop(h * size, (h + 1) * size, one, 0, unroll=True)

    def pair_terms(b, h):
        sibling(b + twin, h).wait_recv()
        add_terms((b, b + twin), h)

    def terms(t, h):
        @pl.when(z >= t)
        def _():
            pair_terms(me_d - 2 * t, h)

        @pl.when(z + t < nz)
        def _():
            pair_terms(me_d + 2 * t, h)

    def rows_back(h):
        for t in range(1, space):
            ag_arrival(t, h).wait_recv()
        for g in range(groups):
            mixed = jnp.concatenate([iall[h, :, g * GROUP + i, :] for i in range(GROUP)], axis=1)
            turned = jnp.concatenate(
                [-sign * turn(mixed[:, i * lanes : (i + 1) * lanes]) for i in range(GROUP)],
                axis=1,
            )
            high, low = split(jnp.concatenate([mixed, turned], axis=0))
            found = jnp.dot(
                rows_out[h],
                jnp.concatenate([high, low], axis=0),
                preferred_element_type=jnp.float32,
            )
            found = found[:rows] + found[rows:]
            place = pl.ds(g * GROUP * lanes, GROUP * lanes)
            if h == 0:
                back_sum[:, place] = found
            else:
                found = back_sum[:, place] + found
                high, low = split(
                    jnp.concatenate(
                        [found[:, i * lanes : (i + 1) * lanes] for i in range(GROUP)], axis=0
                    )
                )
                place = pl.ds(g * GROUP * rows, GROUP * rows)
                back_ref[place, pl.ds(0, lanes)] = high
                back_ref[place, pl.ds(lanes, lanes)] = low
                back_store(g).start()

    def back_store(g):
        place = pl.ds(g * GROUP * rows, GROUP * rows)
        return pltpu.make_async_copy(back_ref.at[place], back_hbm.at[place], store_sem.at[g])

    def gw_store(h):
        place = pl.ds(h * size, size)
        return pltpu.make_async_copy(
            gw_ref.at[place], gw_hbm.at[place], store_sem.at[groups + h]
        )

    for t in range(1, space):
        for piece in range(groups):
            rs_copy(t, piece).wait_recv()
    summed(0)
    l_w.wait()
    mixed_by(0)
    ag_start(0)
    forward(1, 0)
    for t in range(1, dp):
        sp_arrival(t).wait_recv()
    for b in range(dp):
        rows_of(b)
    for t in range(1, space):
        rs_copy(t, groups).wait_recv()
    summed(1)
    mixed_by(1)
    ag_start(1)
    if nz > 2:
        forward(2, 0)
    pair_terms(me_d, 0)
    pair_terms(me_d, 1)
    forward(1, 1)
    terms(1, 0)
    if nz > 3:
        forward(3, 0)
    if nz > 2:
        forward(2, 1)
    l_rows_out.wait()
    rows_back(0)
    terms(1, 1)
    if nz > 2:
        terms(2, 0)
    if nz > 3:
        terms(3, 0)
        forward(3, 1)
    rows_back(1)
    if nz > 2:
        terms(2, 1)
    if nz > 3:
        terms(3, 1)
    for t in range(4, nz):
        for h in range(2):
            forward(t, h)
            terms(t, h)
    for h in range(2):
        gw_store(h).start()

    def leave(copy):
        copy.wait_send()

    for t in range(1, space):
        for piece in range(groups + 1):
            rs_copy(t, piece).wait_send()
        for h in range(2):
            ag_copy(t, h).wait_send()
    for t in range(1, dp):
        sp_copy(t).wait_send()
    for h in range(2):
        own_sends(h, leave)
        for t in range(1, nz):
            passed_on(t, h, leave, False)
    for g in range(groups):
        back_store(g).wait()
    for h in range(2):
        gw_store(h).wait()


def columns_kernel(
    back_hbm, terms_hbm, out_of_hbm, gin_hbm, gw_hbm,
    back, terms, out_of, gin, load_sem, store_sem,
):
    channels, rows, cols = gin.shape
    groups = channels // GROUP
    lanes = back.shape[1] // 2
    count = GROUP * rows
    l_out_of = pltpu.make_async_copy(out_of_hbm, out_of, load_sem.at[groups])
    l_out_of.start()
    loads, stores = [], []
    for g in range(groups):
        place = pl.ds(g * count, count)
        loads.append(pltpu.make_async_copy(back_hbm.at[place], back.at[place], load_sem.at[g]))
        loads[g].start()
    l_terms = pltpu.make_async_copy(terms_hbm, terms, load_sem.at[groups + 1])
    l_terms.start()
    l_out_of.wait()
    for g in range(groups):
        loads[g].wait()
        both = back[pl.ds(g * count, count)]
        raster = jnp.dot(
            jnp.concatenate([both, both[:, :lanes]], axis=1),
            out_of[...],
            preferred_element_type=jnp.float32,
        )
        place = pl.ds(g * GROUP, GROUP)
        gin[place] = raster.reshape(GROUP, rows, cols).astype(jnp.bfloat16)
        stores.append(pltpu.make_async_copy(gin.at[place], gin_hbm.at[0, place], store_sem.at[g]))
        stores[g].start()
        if g == 0:
            l_terms.wait()
            s_terms = pltpu.make_async_copy(terms, gw_hbm, store_sem.at[groups])
            s_terms.start()
    for store in stores:
        store.wait()
    s_terms.wait()


def fused_body(dp, space, cotangent, spectrum, weights):
    _, channels, rows, cols = cotangent.shape
    local, _, _, lanes = spectrum.shape
    modes = local * space
    own = channels // dp
    groups = channels // GROUP
    fixed = [jnp.asarray(t) for t in tables(modes, lanes // 2, rows, cols, space)]
    into, rows_in, rows_out, out_of = fixed
    f32 = jnp.float32
    dma = pltpu.SemaphoreType.DMA
    back, terms = pl.pallas_call(
        functools.partial(kernel, dp, space),
        out_shape=(
            jax.ShapeDtypeStruct((channels * rows, 2 * lanes), jnp.bfloat16),
            jax.ShapeDtypeStruct((local, own * channels, lanes), f32),
        ),
        in_specs=[pl.BlockSpec(memory_space=pl.ANY)] * 6,
        out_specs=[pl.BlockSpec(memory_space=pl.ANY)] * 2,
        scratch_shapes=[
            pltpu.VMEM((channels * rows, 2 * lanes), jnp.bfloat16),
            pltpu.VMEM((local, own * channels, lanes), f32),
            pltpu.VMEM((channels, rows, cols), jnp.bfloat16),
            pltpu.VMEM((local, channels, lanes), f32),
            pltpu.VMEM(weights.shape, f32),
            pltpu.VMEM(into.shape, jnp.bfloat16),
            pltpu.VMEM(rows_in.shape[1:], jnp.bfloat16),
            pltpu.VMEM(rows_out.shape[1:], jnp.bfloat16),
            pltpu.VMEM((modes, channels, lanes), f32),
            pltpu.VMEM((space - 1, local, channels, lanes), f32),
            pltpu.VMEM((dp, local, channels, lanes), f32),
            pltpu.VMEM((2, modes // 2, channels, lanes), f32),
            pltpu.VMEM((rows, channels * lanes), f32),
            pltpu.VMEM((dp, local * own, lanes), f32),
            pltpu.VMEM((dp, local * own, lanes), f32),
            pltpu.VMEM((dp, local * own, lanes), f32),
            pltpu.VMEM((dp, local * own, lanes), f32),
            dma((groups + 5,)),
            dma((groups + 2,)),
            dma((space - 1, groups + 1)),
            dma((space - 1, groups + 1)),
            dma((space - 1, 2)),
            dma((space - 1, 2)),
            dma((dp,)),
            dma((dp,)),
            dma((dp, 2)),
            dma((dp, 2)),
            dma((dp, 2)),
            dma((dp, 2)),
        ],
        compiler_params=pltpu.CompilerParams(
            collective_id=0, has_side_effects=True, vmem_limit_bytes=62 * 1024 * 1024
        ),
    )(cotangent, spectrum, weights, into, rows_in, rows_out)
    return pl.pallas_call(
        columns_kernel,
        out_shape=(
            jax.ShapeDtypeStruct(cotangent.shape, jnp.bfloat16),
            jax.ShapeDtypeStruct(terms.shape, f32),
        ),
        in_specs=[pl.BlockSpec(memory_space=pl.ANY)] * 3,
        out_specs=[pl.BlockSpec(memory_space=pl.ANY)] * 2,
        scratch_shapes=[
            pltpu.VMEM(back.shape, jnp.bfloat16),
            pltpu.VMEM(terms.shape, f32),
            pltpu.VMEM(out_of.shape, jnp.bfloat16),
            pltpu.VMEM(cotangent.shape[1:], jnp.bfloat16),
            dma((groups + 2,)),
            dma((groups + 1,)),
        ],
        compiler_params=pltpu.CompilerParams(vmem_limit_bytes=62 * 1024 * 1024),
    )(back, terms, out_of)


def solution(mesh):
    placed = (
        P("dp", None, "space", None),
        P("space", "dp", None, None),
        P("space", None, None, None),
    )
    dp, space = mesh.shape["dp"], mesh.shape["space"]

    def body(cotangent, spectrum, weights):
        rasters, channels, rows, _ = cotangent.shape
        whole_rows = (
            rasters == 1
            and dp % 2 == 0
            and channels % dp == 0
            and channels % GROUP == 0
            and spectrum.shape[0] % 2 == 0
            and rows % 16 == 0
            and (spectrum.shape[0] * (channels // dp)) % 8 == 0
        )
        if whole_rows:
            return fused_body(dp, space, cotangent, spectrum, weights)
        return general_body(cotangent, spectrum, weights)

    return jax.shard_map(
        body,
        mesh=mesh,
        in_specs=placed,
        out_specs=(P("dp", None, "space", None), P("space", "dp", None)),
        check_vma=False,
    )
```

```python
import functools
import math

import jax
import jax.numpy as jnp
import ml_dtypes
import numpy as np
from jax import lax
from jax.experimental import pallas as pl
from jax.experimental.pallas import tpu as pltpu
from jax.sharding import PartitionSpec as P

MESH = pl.DeviceIdType.MESH
GROUP = 8


def column_basis(col_count, modes_y):
    position = jnp.arange(col_count, dtype=jnp.int32)
    frequency = jnp.arange(modes_y, dtype=jnp.int32)
    phase = position[:, None] * frequency[None, :] % col_count
    angles = phase.astype(jnp.float32) * (2.0 * math.pi / col_count)
    return jnp.concatenate([jnp.cos(angles), -jnp.sin(angles)], axis=1)


def row_basis(mode_count, first_row, row_count, height):
    frequency = jnp.arange(mode_count, dtype=jnp.int32)
    position = first_row + jnp.arange(row_count, dtype=jnp.int32)
    phase = frequency[:, None] * position[None, :] % height
    angles = phase.astype(jnp.float32) * (2.0 * math.pi / height)
    return (jnp.cos(angles), jnp.sin(angles))


def spectral_backward(spec_grad, weights, modes_y):
    hp = lax.Precision.HIGHEST
    grad_re, grad_im = (spec_grad[..., :modes_y], spec_grad[..., modes_y:])
    weight_re, weight_im = (weights[..., :modes_y], weights[..., modes_y:])
    real_part = jnp.einsum("kbox,kcox->kbcx", grad_re, weight_re, precision=hp) + jnp.einsum(
        "kbox,kcox->kbcx", grad_im, weight_im, precision=hp
    )
    imag_part = jnp.einsum("kbox,kcox->kbcx", grad_im, weight_re, precision=hp) - jnp.einsum(
        "kbox,kcox->kbcx", grad_re, weight_im, precision=hp
    )
    return jnp.concatenate([real_part, imag_part], axis=-1)


def weight_terms(spectrum, spec_grad, modes_y):
    hp = lax.Precision.HIGHEST
    spec_re, spec_im = (spectrum[..., :modes_y], spectrum[..., modes_y:])
    grad_re, grad_im = (spec_grad[..., :modes_y], spec_grad[..., modes_y:])
    real_part = jnp.einsum("kbcx,kbox->kcox", spec_re, grad_re, precision=hp) + jnp.einsum(
        "kbcx,kbox->kcox", spec_im, grad_im, precision=hp
    )
    imag_part = jnp.einsum("kbcx,kbox->kcox", spec_re, grad_im, precision=hp) - jnp.einsum(
        "kbcx,kbox->kcox", spec_im, grad_re, precision=hp
    )
    joined = jnp.concatenate([real_part, imag_part], axis=-1)
    return joined.reshape(joined.shape[0], joined.shape[1] * joined.shape[2], joined.shape[3])


def general_body(cotangent, spectrum, weights):
    hp = lax.Precision.HIGHEST
    space_count = lax.axis_size("space")
    raster_count, channels, row_count, col_count = cotangent.shape
    local_modes = spectrum.shape[0]
    modes_y = spectrum.shape[3] // 2
    height = row_count * space_count
    basis = column_basis(col_count, modes_y)
    first_row = lax.axis_index("space") * row_count
    col_spec = jnp.einsum(
        "rcxw,wj->rcxj", cotangent, basis, precision=hp, preferred_element_type=jnp.float32
    )
    forward_scale = 1.0 / math.sqrt(height * col_count)
    cosines, sines = row_basis(local_modes * lax.axis_size("space"), first_row, row_count, height)
    with_cos = jnp.einsum("kx,rcxj->krcj", cosines, col_spec, precision=hp)
    with_sin = jnp.einsum("kx,rcxj->krcj", sines, col_spec, precision=hp)
    joined = jnp.concatenate(
        [
            with_cos[..., :modes_y] + with_sin[..., modes_y:],
            with_cos[..., modes_y:] - with_sin[..., :modes_y],
        ],
        axis=-1,
    )
    spec_grad = lax.psum_scatter(joined * forward_scale, "space", scatter_dimension=0, tiled=True)
    input_spec = spectral_backward(spec_grad, weights, modes_y)
    local_terms = weight_terms(spectrum, spec_grad, modes_y)
    grad_weights = lax.psum_scatter(local_terms, "dp", scatter_dimension=1, tiled=True)
    shard_piece = lax.all_gather(input_spec, "space", axis=0, tiled=True)
    cosines, sines = row_basis(shard_piece.shape[0], first_row, row_count, height)
    back_cos = jnp.einsum("kx,krcj->rcxj", cosines, shard_piece, precision=hp)
    back_sin = jnp.einsum("kx,krcj->rcxj", sines, shard_piece, precision=hp)
    joined = jnp.concatenate(
        [
            back_cos[..., :modes_y] - back_sin[..., modes_y:],
            back_cos[..., modes_y:] + back_sin[..., :modes_y],
        ],
        axis=-1,
    )
    inverse_scale = 1.0 / math.sqrt(local_modes * space_count * modes_y)
    grad_input = (jnp.einsum("rcxj,wj->rcxw", joined, basis, precision=hp) * inverse_scale).astype(
        jnp.bfloat16
    )
    return (grad_input, grad_weights)


def halves(table):
    high = table.astype(ml_dtypes.bfloat16)
    low = (table - high.astype(np.float64)).astype(ml_dtypes.bfloat16)
    return high, low


def stack(high, low):
    above = np.concatenate([high, high], axis=-1)
    below = np.concatenate([low, np.zeros_like(low)], axis=-1)
    return np.concatenate([above, below], axis=-2)


def tables(modes, modes_y, rows, cols, space):
    height = rows * space
    angle = 2.0 * np.pi * (np.outer(np.arange(cols), np.arange(modes_y)) % cols) / cols
    high, low = halves(np.concatenate([np.cos(angle), -np.sin(angle)], axis=1))
    into = np.concatenate([high, low], axis=1)
    out_of = np.concatenate([high.T, high.T, low.T], axis=0)
    angle = 2.0 * np.pi * (np.outer(np.arange(modes), np.arange(height)) % height) / height
    cosines = np.cos(angle).reshape(modes, space, rows).transpose(1, 0, 2)
    sines = np.sin(angle).reshape(modes, space, rows).transpose(1, 0, 2)
    high, low = halves(np.concatenate([cosines, sines], axis=2) / math.sqrt(height * cols))
    rows_in = stack(high, low)
    local = modes // space
    order = np.arange(modes).reshape(space, 2, local // 2).transpose(1, 0, 2).reshape(2, -1)
    both = np.concatenate([cosines[:, order], sines[:, order]], axis=2).transpose(0, 1, 3, 2)
    high, low = halves(both / math.sqrt(modes * modes_y))
    rows_out = stack(high, low)
    return into, rows_in, rows_out, out_of


def split(values):
    high = values.astype(jnp.bfloat16)
    low = (values - high.astype(jnp.float32)).astype(jnp.bfloat16)
    return high, low


def kernel(
    dp, space,
    cot_hbm, spec_hbm, w_hbm, into_hbm, rows_in_hbm, rows_out_hbm, out_of_hbm,
    back_hbm, gw_hbm,
    back_ref, gw_ref, cot, spec, w, into, rows_in, rows_out, out_of,
    part, rs_in, gall, iall, back_sum, sp_out, sp_in, a_rows, b_rows,
    load_sem, store_sem, rs_send, rs_recv, ag_send, ag_recv, sp_send, sp_recv,
    up_send, down_send, sib_send, g_recv,
):
    me_d = lax.axis_index("dp")
    me_s = lax.axis_index("space")
    channels, rows, cols = cot.shape
    local = w.shape[0]
    modes = local * space
    lanes = w.shape[3]
    half = lanes // 2
    own = channels // dp
    groups = channels // GROUP

    def at(d, s):
        return {"dp": d, "space": s}

    def partner_d(t):
        return lax.rem(me_d + t, dp)

    def partner_s(t):
        return lax.rem(me_s + t, space)

    def source_s(t):
        return lax.rem(me_s + space - t, space)

    barrier = pltpu.get_barrier_semaphore()
    for t in range(1, dp):
        pl.semaphore_signal(barrier, inc=1, device_id=at(partner_d(t), me_s), device_id_type=MESH)
    for t in range(1, space):
        pl.semaphore_signal(barrier, inc=1, device_id=at(me_d, partner_s(t)), device_id_type=MESH)

    def load(n, src, dst):
        copy = pltpu.make_async_copy(src, dst, load_sem.at[n])
        copy.start()
        return copy

    l_into = load(0, into_hbm, into)
    l_cot = []
    for g in range(groups):
        place = pl.ds(g * GROUP, GROUP)
        l_cot.append(load(1 + g, cot_hbm.at[0, place], cot.at[place]))
    n = 1 + groups
    l_rows_in = load(n, rows_in_hbm.at[me_s], rows_in)
    l_spec = load(n + 1, spec_hbm.at[:, 0], spec)
    l_w = load(n + 2, w_hbm, w)
    l_rows_out = load(n + 3, rows_out_hbm.at[me_s], rows_out)
    l_out_of = load(n + 4, out_of_hbm, out_of)

    lane = lax.broadcasted_iota(jnp.int32, (1, lanes), 1)
    lower = lane < half
    sign = jnp.where(lower, 1.0, -1.0).astype(jnp.float32)

    def turn(values):
        return pltpu.roll(values, half, values.ndim - 1)

    size = local // 2

    def rs_copy(t, piece):
        there = partner_s(t)
        if piece < groups:
            first, place = 0, pl.ds(piece * GROUP, GROUP)
        else:
            first, place = size, pl.ds(0, channels)
        return pltpu.make_async_remote_copy(
            part.at[pl.ds(there * local + first, size), place],
            rs_in.at[t - 1, pl.ds(first, size), place],
            rs_send.at[t - 1, piece],
            rs_recv.at[t - 1, piece],
            device_id=at(me_d, there),
            device_id_type=MESH,
        )

    def sp_copy(t):
        there = partner_d(t)
        return pltpu.make_async_remote_copy(
            sp_out.at[there],
            sp_in.at[me_d],
            sp_send.at[t],
            sp_recv.at[t],
            device_id=at(there, me_s),
            device_id_type=MESH,
        )

    def sp_arrival(t):
        source = lax.rem(me_d + dp - t, dp)
        return pltpu.make_async_remote_copy(
            sp_out.at[source],
            sp_in.at[source],
            sp_send.at[t],
            sp_recv.at[t],
            device_id=at(source, me_s),
            device_id_type=MESH,
        )

    def send_spectrum():
        l_spec.wait()
        for d in range(dp):
            for k in range(local):
                sp_out[d, k * own : (k + 1) * own, :] = spec[k, d * own : (d + 1) * own, :]
        for t in range(1, dp):
            sp_copy(t).start()
        sp_in[me_d] = sp_out[me_d]

    l_into.wait()
    l_rows_in.wait()
    for g in range(groups):
        l_cot[g].wait()
        block = cot[pl.ds(g * GROUP, GROUP)].reshape(GROUP * rows, cols)
        both = jnp.dot(block, into[...], preferred_element_type=jnp.float32)
        col = both[:, :lanes] + both[:, lanes:]
        turned = turn(col) * sign
        stacked = jnp.concatenate(
            [
                jnp.concatenate(
                    [col[i * rows : (i + 1) * rows], turned[i * rows : (i + 1) * rows]], axis=0
                )
                for i in range(GROUP)
            ],
            axis=1,
        )
        high, low = split(stacked)
        spectrum_part = jnp.dot(
            rows_in[...],
            jnp.concatenate([high, low], axis=0),
            preferred_element_type=jnp.float32,
        )
        spectrum_part = spectrum_part[:modes] + spectrum_part[modes:]
        for i in range(GROUP):
            part[:, g * GROUP + i, :] = spectrum_part[:, i * lanes : (i + 1) * lanes]
        if g == 0:
            pl.semaphore_wait(barrier, dp + space - 2)
        for t in range(1, space):
            rs_copy(t, g).start()
        if g == 0:
            send_spectrum()
    for t in range(1, space):
        rs_copy(t, groups).start()

    gw_ref[...] = jnp.zeros_like(gw_ref)

    z, core = me_d // 2, lax.rem(me_d, 2)
    nz = dp // 2
    twin = 1 - 2 * core

    def g_copy(b, h, there, sem):
        place = pl.ds(h * size, size)
        return pltpu.make_async_remote_copy(
            gall.at[b, place],
            gall.at[b, place],
            sem.at[b, h],
            g_recv.at[b, h],
            device_id=at(there, me_s),
            device_id_type=MESH,
        )

    def up(b, h):
        return g_copy(b, h, me_d + 2, up_send)

    def down(b, h):
        return g_copy(b, h, me_d - 2, down_send)

    def sibling(b, h):
        return g_copy(b, h, me_d + twin, sib_send)

    def own_sends(h, act):
        @pl.when(z < nz - 1)
        def _():
            act(up(me_d, h))

        @pl.when(z > 0)
        def _():
            act(down(me_d, h))

        act(sibling(me_d, h))

    def passed_on(t, h, act, arrive):
        @pl.when(z >= t)
        def _():
            below = me_d - 2 * t
            if arrive:
                down(below, h).wait_recv()

            @pl.when(z < nz - 1)
            def _():
                act(up(below, h))

            act(sibling(below, h))

        @pl.when(z + t < nz)
        def _():
            above = me_d + 2 * t
            if arrive:
                up(above, h).wait_recv()

            @pl.when(z > 0)
            def _():
                act(down(above, h))

            act(sibling(above, h))

    def forward(t, h):
        passed_on(t, h, lambda copy: copy.start(), True)

    def ag_copy(t, h):
        place = pl.ds(me_s * size, size)
        return pltpu.make_async_remote_copy(
            iall.at[h, place],
            iall.at[h, place],
            ag_send.at[t - 1, h],
            ag_recv.at[t - 1, h],
            device_id=at(me_d, partner_s(t)),
            device_id_type=MESH,
        )

    def ag_arrival(t, h):
        place = pl.ds(source_s(t) * size, size)
        return pltpu.make_async_remote_copy(
            iall.at[h, place],
            iall.at[h, place],
            ag_send.at[t - 1, h],
            ag_recv.at[t - 1, h],
            device_id=at(me_d, source_s(t)),
            device_id_type=MESH,
        )

    def summed(h):
        def gather_sum(k, carry):
            total = part[me_s * local + k]
            for t in range(1, space):
                total = total + rs_in[t - 1, k]
            gall[me_d, k] = total
            return carry

        lax.fori_loop(h * size, (h + 1) * size, gather_sum, 0, unroll=True)
        own_sends(h, lambda copy: copy.start())

    def mixed_by(h):
        def mix(k, carry):
            grad = gall[me_d, k]
            weight = w[k]
            plain = jnp.sum(weight * grad[None], axis=1)
            cross = jnp.sum(weight * turn(grad)[None], axis=1)
            mixed = jnp.where(lower, plain + turn(plain), turn(cross) - cross)
            iall[h, me_s * size + k - h * size] = mixed
            return carry

        lax.fori_loop(h * size, (h + 1) * size, mix, 0, unroll=True)

    def ag_start(h):
        for t in range(1, space):
            ag_copy(t, h).start()

    def rows_of(b):
        saved = sp_in[b]
        a_rows[b] = jnp.where(lower, saved, turn(saved))
        b_rows[b] = jnp.where(lower, turn(saved), -saved)

    def add_terms(blocks, h):
        def one(k, carry):
            grads = [gall[b, k] for b in blocks]
            turned = [turn(grad) for grad in grads]
            for c in range(own):
                row = pl.ds(k * own + c, 1)
                place = pl.ds(c * channels, channels)
                total = gw_ref[k, place, :]
                for b, grad, other in zip(blocks, grads, turned):
                    total = total + (a_rows[b, row, :] * grad + b_rows[b, row, :] * other)
                gw_ref[k, place, :] = total
            return carry

        lax.fori_loop(h * size, (h + 1) * size, one, 0, unroll=True)

    def pair_terms(b, h):
        sibling(b + twin, h).wait_recv()
        add_terms((b, b + twin), h)

    def terms(t, h):
        @pl.when(z >= t)
        def _():
            pair_terms(me_d - 2 * t, h)

        @pl.when(z + t < nz)
        def _():
            pair_terms(me_d + 2 * t, h)

    def rows_back(h):
        for t in range(1, space):
            ag_arrival(t, h).wait_recv()
        for g in range(groups):
            mixed = jnp.concatenate([iall[h, :, g * GROUP + i, :] for i in range(GROUP)], axis=1)
            turned = jnp.concatenate(
                [-sign * turn(mixed[:, i * lanes : (i + 1) * lanes]) for i in range(GROUP)],
                axis=1,
            )
            high, low = split(jnp.concatenate([mixed, turned], axis=0))
            found = jnp.dot(
                rows_out[h],
                jnp.concatenate([high, low], axis=0),
                preferred_element_type=jnp.float32,
            )
            found = found[:rows] + found[rows:]
            place = pl.ds(g * GROUP * lanes, GROUP * lanes)
            if h == 0:
                back_sum[:, place] = found
            else:
                found = back_sum[:, place] + found
                high, low = split(
                    jnp.concatenate(
                        [found[:, i * lanes : (i + 1) * lanes] for i in range(GROUP)], axis=0
                    )
                )
                raster = jnp.dot(
                    jnp.concatenate([high, low, high], axis=1),
                    out_of[...],
                    preferred_element_type=jnp.float32,
                )
                back_ref[pl.ds(g * GROUP, GROUP)] = raster.reshape(GROUP, rows, cols).astype(
                    jnp.bfloat16
                )
                back_store(g).start()

    def back_store(g):
        place = pl.ds(g * GROUP, GROUP)
        return pltpu.make_async_copy(back_ref.at[place], back_hbm.at[0, place], store_sem.at[g])

    def gw_store(h):
        place = pl.ds(h * size, size)
        return pltpu.make_async_copy(
            gw_ref.at[place], gw_hbm.at[place], store_sem.at[groups + h]
        )

    for t in range(1, space):
        for piece in range(groups):
            rs_copy(t, piece).wait_recv()
    summed(0)
    l_w.wait()
    mixed_by(0)
    ag_start(0)
    forward(1, 0)
    for t in range(1, dp):
        sp_arrival(t).wait_recv()
    for b in range(dp):
        rows_of(b)
    for t in range(1, space):
        rs_copy(t, groups).wait_recv()
    summed(1)
    mixed_by(1)
    ag_start(1)
    if nz > 2:
        forward(2, 0)
    pair_terms(me_d, 0)
    pair_terms(me_d, 1)
    forward(1, 1)
    terms(1, 0)
    if nz > 3:
        forward(3, 0)
    if nz > 2:
        forward(2, 1)
    l_rows_out.wait()
    rows_back(0)
    terms(1, 1)
    if nz > 2:
        terms(2, 0)
    if nz > 3:
        terms(3, 0)
        forward(3, 1)
    l_out_of.wait()
    rows_back(1)
    if nz > 2:
        terms(2, 1)
    if nz > 3:
        terms(3, 1)
    for t in range(4, nz):
        for h in range(2):
            forward(t, h)
            terms(t, h)
    for h in range(2):
        gw_store(h).start()

    def leave(copy):
        copy.wait_send()

    for t in range(1, space):
        for piece in range(groups + 1):
            rs_copy(t, piece).wait_send()
        for h in range(2):
            ag_copy(t, h).wait_send()
    for t in range(1, dp):
        sp_copy(t).wait_send()
    for h in range(2):
        own_sends(h, leave)
        for t in range(1, nz):
            passed_on(t, h, leave, False)
    for g in range(groups):
        back_store(g).wait()
    for h in range(2):
        gw_store(h).wait()


def store_kernel(gin_hbm, terms_hbm, gin_out, gw_out, sem):
    copies = [pltpu.make_async_copy(terms_hbm, gw_out, sem.at[0])]
    channels = gin_hbm.shape[1]
    for g in range(channels // GROUP):
        place = pl.ds(g * GROUP, GROUP)
        copies.append(
            pltpu.make_async_copy(gin_hbm.at[0, place], gin_out.at[0, place], sem.at[1 + g])
        )
    for copy in copies:
        copy.start()
    for copy in copies:
        copy.wait()


def fused_body(dp, space, cotangent, spectrum, weights):
    _, channels, rows, cols = cotangent.shape
    local, _, _, lanes = spectrum.shape
    modes = local * space
    own = channels // dp
    groups = channels // GROUP
    fixed = [jnp.asarray(t) for t in tables(modes, lanes // 2, rows, cols, space)]
    into, rows_in, rows_out, out_of = fixed
    f32 = jnp.float32
    dma = pltpu.SemaphoreType.DMA
    back, terms = pl.pallas_call(
        functools.partial(kernel, dp, space),
        out_shape=(
            jax.ShapeDtypeStruct(cotangent.shape, jnp.bfloat16),
            jax.ShapeDtypeStruct((local, own * channels, lanes), f32),
        ),
        in_specs=[pl.BlockSpec(memory_space=pl.ANY)] * 7,
        out_specs=[pl.BlockSpec(memory_space=pl.ANY)] * 2,
        scratch_shapes=[
            pltpu.VMEM((channels, rows, cols), jnp.bfloat16),
            pltpu.VMEM((local, own * channels, lanes), f32),
            pltpu.VMEM((channels, rows, cols), jnp.bfloat16),
            pltpu.VMEM((local, channels, lanes), f32),
            pltpu.VMEM(weights.shape, f32),
            pltpu.VMEM(into.shape, jnp.bfloat16),
            pltpu.VMEM(rows_in.shape[1:], jnp.bfloat16),
            pltpu.VMEM(rows_out.shape[1:], jnp.bfloat16),
            pltpu.VMEM(out_of.shape, jnp.bfloat16),
            pltpu.VMEM((modes, channels, lanes), f32),
            pltpu.VMEM((space - 1, local, channels, lanes), f32),
            pltpu.VMEM((dp, local, channels, lanes), f32),
            pltpu.VMEM((2, modes // 2, channels, lanes), f32),
            pltpu.VMEM((rows, channels * lanes), f32),
            pltpu.VMEM((dp, local * own, lanes), f32),
            pltpu.VMEM((dp, local * own, lanes), f32),
            pltpu.VMEM((dp, local * own, lanes), f32),
            pltpu.VMEM((dp, local * own, lanes), f32),
            dma((groups + 6,)),
            dma((groups + 2,)),
            dma((space - 1, groups + 1)),
            dma((space - 1, groups + 1)),
            dma((space - 1, 2)),
            dma((space - 1, 2)),
            dma((dp,)),
            dma((dp,)),
            dma((dp, 2)),
            dma((dp, 2)),
            dma((dp, 2)),
            dma((dp, 2)),
        ],
        compiler_params=pltpu.CompilerParams(
            collective_id=0, has_side_effects=True, vmem_limit_bytes=62 * 1024 * 1024
        ),
    )(cotangent, spectrum, weights, into, rows_in, rows_out, out_of)
    return pl.pallas_call(
        store_kernel,
        out_shape=(
            jax.ShapeDtypeStruct(cotangent.shape, jnp.bfloat16),
            jax.ShapeDtypeStruct(terms.shape, f32),
        ),
        in_specs=[pl.BlockSpec(memory_space=pl.ANY)] * 2,
        out_specs=[pl.BlockSpec(memory_space=pl.ANY)] * 2,
        scratch_shapes=[dma((groups + 1,))],
        compiler_params=pltpu.CompilerParams(vmem_limit_bytes=62 * 1024 * 1024),
    )(back, terms)


def solution(mesh):
    placed = (
        P("dp", None, "space", None),
        P("space", "dp", None, None),
        P("space", None, None, None),
    )
    dp, space = mesh.shape["dp"], mesh.shape["space"]

    def body(cotangent, spectrum, weights):
        rasters, channels, rows, _ = cotangent.shape
        whole_rows = (
            rasters == 1
            and dp % 2 == 0
            and channels % dp == 0
            and channels % GROUP == 0
            and spectrum.shape[0] % 2 == 0
            and rows % 16 == 0
            and (spectrum.shape[0] * (channels // dp)) % 8 == 0
        )
        if whole_rows:
            return fused_body(dp, space, cotangent, spectrum, weights)
        return general_body(cotangent, spectrum, weights)

    return jax.shard_map(
        body,
        mesh=mesh,
        in_specs=placed,
        out_specs=(P("dp", None, "space", None), P("space", "dp", None)),
        check_vma=False,
    )
```
